512 devices in a mesh: lon: 64 (over x, z), lat: 8 (over y, core).
Axes of the slice: x: 4, y: 4, z: 16, core: 2. Of those that a mesh axis runs over, the one named last changes fastest.
Arguments:
- right_side: float32 [16, 64, 32768], P(None, 'lat', 'lon'), may hold values from -6 to 6
- initial_guess: float32 [16, 64, 32768], P(None, 'lat', 'lon'), may hold values from -3 to 3
- land_mask: float32 [16, 64, 32768], P(None, 'lat', 'lon'), may hold values from 0 to 1
- coefficient_sets: float32 [2, 4, 16], replicated, may hold values from 0.05 to 1
Outputs:
- iterate: float32 [16, 64, 32768], P(None, 'lat', 'lon')
- residual: float32 [16, 64, 32768], P(None, 'lat', 'lon')
- direction: float32 [16, 64, 32768], P(None, 'lat', 'lon')
The draws below stay inside these ranges and needn't reach their ends.
All inputs are finite; a program needn't handle non-finite values.
Results may differ from the reference program's by a relative error of at most 0.0028.
Values sent between devices are 32-bit elements; how exact they have to be, the bound alone decides.
No kernel may reach another device: no remote copies, remote signals or barrier semaphores. Data moves between devices by JAX's collectives and lax.ppermute only.
A program may use at most 64 MiB of HBM per device.

```python
import math
import jax
import jax.numpy as jnp

LEV = 16
COARSE_SWEEPS = 4
NLON = 32768
NLAT = 64


def shard_levels(key, extent, split, low, largest):
    gain = 1.0
    for position, shards_of in split:
        heights = jax.random.uniform(jax.random.fold_in(jax.random.fold_in(key, 6), position), (shards_of,), jnp.float32, low / len(split), largest / len(split))
        gain = gain * jnp.repeat(jnp.exp(heights), extent[position] // shards_of).reshape((-1,) + (1,) * (len(extent) - 1 - position))
    return gain


def scatter_about(stream_key, dims, deviation, limit, cuts=(), dtype=jnp.bfloat16):
    drawn = jax.random.normal(stream_key, dims, jnp.float32) * deviation
    if len(cuts) > 0:
        drawn = shard_levels(stream_key, dims, cuts, -0.22, 0.18) * drawn
    return jnp.clip(drawn, min=-limit, max=limit).astype(dtype)


def setup_inputs(seed: int = 0) -> dict:
    key_of = jax.random.split(jax.random.key(seed), 5)
    return {
        "right_side": scatter_about(key_of[0], (LEV, NLAT, NLON), 1.0, 6.0, ((1, 8), (2, 64)), jnp.float32),
        "initial_guess": scatter_about(key_of[1], (LEV, NLAT, NLON), 0.5, 3.0, ((1, 8), (2, 64)), jnp.float32),
        "land_mask": jnp.clip(1.0 * jax.random.uniform(key_of[2], (LEV, NLAT, NLON), jnp.float32) ** shard_levels(key_of[2], (LEV, NLAT, NLON), ((1, 8), (2, 64)), -0.2, 0.2), 0.0, 1.0),
        "coefficient_sets": jnp.clip(jnp.exp(jax.random.uniform(key_of[3], (2, 4, LEV), jnp.float32, math.log(0.05), math.log(1.0))), 0.05, 1.0),
    }


relax_factor = 0.8


def blend_set(land_share, coefficient_sets, column):
    sea_value = coefficient_sets[0, column][:, None, None]
    land_value = coefficient_sets[1, column][:, None, None]
    return sea_value + land_share * (land_value - sea_value)


def fine_coefficients(land_mask, coefficient_sets):
    reaction = blend_set(land_mask, coefficient_sets, 0)
    lon_weight = blend_set(land_mask, coefficient_sets, 1)
    lat_weight = blend_set(land_mask, coefficient_sets, 2)
    lev_weight = blend_set(land_mask, coefficient_sets, 3)
    face_east = 0.5 * (lon_weight + jnp.roll(lon_weight, -1, axis=2))
    face_west = 0.5 * (lon_weight + jnp.roll(lon_weight, 1, axis=2))
    lat_pad = jnp.pad(lat_weight, ((0, 0), (1, 1), (0, 0)))
    face_north = 0.5 * (lat_weight + lat_pad[:, 2:, :])
    face_south = 0.5 * (lat_weight + lat_pad[:, :-2, :])
    lev_pad = jnp.pad(lev_weight, ((1, 1), (0, 0), (0, 0)))
    face_upper = 0.5 * (lev_weight + lev_pad[2:])
    face_lower = 0.5 * (lev_weight + lev_pad[:-2])
    return (reaction, face_east, face_west, face_north, face_south, face_upper, face_lower)


def mean_four(blocks):
    return 0.25 * (blocks[:, 0::2, 0::2] + blocks[:, 0::2, 1::2] + blocks[:, 1::2, 0::2] + blocks[:, 1::2, 1::2])


def coarsen(coeffs):
    reaction, face_east, face_west, face_north, face_south, face_upper, face_lower = coeffs
    east_coarse = 0.25 * (face_east[:, 0::2, 1::2] + face_east[:, 1::2, 1::2])
    west_coarse = 0.25 * (face_west[:, 0::2, 0::2] + face_west[:, 1::2, 0::2])
    north_coarse = 0.25 * (face_north[:, 1::2, 0::2] + face_north[:, 1::2, 1::2])
    south_coarse = 0.25 * (face_south[:, 0::2, 0::2] + face_south[:, 0::2, 1::2])
    return (mean_four(reaction), east_coarse, west_coarse, north_coarse, south_coarse, mean_four(face_upper), mean_four(face_lower))


def diagonal_of(coeffs):
    return coeffs[0] + coeffs[1] + coeffs[2] + coeffs[3] + coeffs[4] + coeffs[5] + coeffs[6]


def prolong(source):
    return jnp.repeat(jnp.repeat(source, 2, axis=1), 2, axis=2)


def operate(source, coeffs):
    reaction, face_east, face_west, face_north, face_south, face_upper, face_lower = coeffs
    lat_pad = jnp.pad(source, ((0, 0), (1, 1), (0, 0)))
    vertical = jnp.pad(source, ((1, 1), (0, 0), (0, 0)))
    applied = reaction * source
    applied = applied + face_east * (source - jnp.roll(source, -1, axis=2))
    applied = applied + face_west * (source - jnp.roll(source, 1, axis=2))
    applied = applied + face_north * (source - lat_pad[:, 2:, :])
    applied = applied + face_south * (source - lat_pad[:, :-2, :])
    applied = applied + face_upper * (source - vertical[2:])
    applied = applied + face_lower * (source - vertical[:-2])
    return applied


def vcycle(rhs_fine, levels):
    fine_coeffs, fine_diag = levels[0]
    mid_coeffs, mid_diag = levels[1]
    coarse_coeffs, coarse_diag = levels[2]
    fine_corr = relax_factor * rhs_fine / fine_diag
    rhs_mid = mean_four(rhs_fine - operate(fine_corr, fine_coeffs))
    mid_corr = relax_factor * rhs_mid / mid_diag
    rhs_coarse = mean_four(rhs_mid - operate(mid_corr, mid_coeffs))
    coarse_corr = relax_factor * rhs_coarse / coarse_diag
    for sweep_index in range(COARSE_SWEEPS - 1):
        coarse_corr = coarse_corr + relax_factor * (rhs_coarse - operate(coarse_corr, coarse_coeffs)) / coarse_diag
    mid_corr = mid_corr + prolong(coarse_corr)
    mid_corr = mid_corr + relax_factor * (rhs_mid - operate(mid_corr, mid_coeffs)) / mid_diag
    fine_corr = fine_corr + prolong(mid_corr)
    fine_corr = fine_corr + relax_factor * (rhs_fine - operate(fine_corr, fine_coeffs)) / fine_diag
    return fine_corr


def reference(right_side, initial_guess, land_mask, coefficient_sets):
    fine_coeffs = fine_coefficients(land_mask, coefficient_sets)
    mid_coeffs = coarsen(fine_coeffs)
    coarse_coeffs = coarsen(mid_coeffs)
    levels = [(fine_coeffs, diagonal_of(fine_coeffs)), (mid_coeffs, diagonal_of(mid_coeffs)), (coarse_coeffs, diagonal_of(coarse_coeffs))]
    start = right_side - operate(initial_guess, fine_coeffs)
    precond = vcycle(start, levels)
    precond_dot = jnp.sum(start * precond)
    image_dir = operate(precond, fine_coeffs)
    curvature = jnp.sum(precond * image_dir)
    step_length = precond_dot / curvature
    iterate = initial_guess + step_length * precond
    residual = start - step_length * image_dir
    precond_next = vcycle(residual, levels)
    next_dot = jnp.sum(residual * precond_next)
    direction = precond_next + (next_dot / precond_dot) * precond
    return iterate, residual, direction
```

```python
import jax
import jax.numpy as jnp
import numpy as np
from jax import lax
from jax.experimental import pallas as pl
from jax.experimental.pallas import tpu as pltpu
from jax.sharding import PartitionSpec as P


LEV = 16
ROWS = 8
OWN = 512
HALF = 64
LANES = OWN + 2 * HALF
RIM = 6
EXT = ROWS + 2 * RIM
MID = EXT // 2
SEND = 5
NEAR = 6
COLS = 256
OWN_COLS = OWN // 4
HALF_COLS = HALF // 4
DAMP = 0.8
KEEP = 1.0 - DAMP
F32 = jnp.float32

VMEM = pl.BlockSpec(memory_space=pltpu.VMEM)
HBM = pl.BlockSpec(memory_space=pltpu.HBM)


def call(body, outs, ins, scratch=(), specs=(), copies=0):
    return pl.pallas_call(
        body,
        out_shape=[jax.ShapeDtypeStruct(o, F32) for o in outs],
        in_specs=list(specs) + [VMEM] * (len(ins) - len(specs)),
        out_specs=[VMEM] * len(outs),
        scratch_shapes=[pltpu.VMEM(s, F32) for s in scratch] + [pltpu.SemaphoreType.DMA((copies,))] * (copies > 0),
        compiler_params=pltpu.CompilerParams(vmem_limit_bytes=(60 if copies else 24) * 1024 * 1024),
        cost_estimate=pl.CostEstimate(flops=1000000, bytes_accessed=1000000, transcendentals=0),
    )(*ins)


def loop(first, end, body, unroll=2):
    def step(i, carry):
        body(i)
        return carry

    lax.fori_loop(first, end, step, 0, unroll=unroll)


def lane_ids():
    return lax.broadcasted_iota(jnp.int32, (LEV, LANES), 1)


def next_lane(v, n=1):
    return pltpu.roll(v, v.shape[-1] - n, axis=1)


def prev_lane(v, n=1):
    return pltpu.roll(v, n, axis=1)


def next_level(v):
    return pltpu.roll(v, LEV - 1, axis=0)


def prev_level(v):
    return pltpu.roll(v, 1, axis=0)


def pair_sum(v, even):
    return v + jnp.where(even, next_lane(v), prev_lane(v))


def around(v, i, east, north, upper, n):
    here = v[i]
    total = east[i] * next_lane(here, n) + prev_lane(east[i] * here, n)
    total = total + upper[i] * next_level(here) + prev_level(upper[i] * here)
    return total + north[i] * v[i + 1] + north[i - 1] * v[i - 1]


def blocks_matrix():
    lane = np.arange(LANES)
    cell = lane // 4
    cell = np.where(cell < OWN_COLS + HALF_COLS, cell, cell + COLS - LANES // 4)
    matrix = np.zeros((LANES, COLS), np.float32)
    matrix[lane, cell] = 1.0
    return jnp.asarray(matrix, jnp.bfloat16)


def times_blocks(rows, blocks, side):
    total = 0.0
    left = rows
    for _ in range(3):
        part = left.astype(jnp.bfloat16)
        left = left - part.astype(F32)
        total = total + lax.dot_general(part, blocks[...], (((1,), (side,)), ((), ())), preferred_element_type=F32)
    return total


def pack_kernel(b_ref, x_ref, c_ref, north_ref, south_ref, east_ref, west_ref, held, turned, arrived):
    low_half = lax.broadcasted_iota(jnp.int32, (LEV, 128), 1) < HALF
    copies = [pltpu.make_async_copy(ref, held.at[j], arrived.at[j]) for j, ref in enumerate((b_ref, x_ref, c_ref))]
    for copy in copies:
        copy.start()
    for j, copy in enumerate(copies):
        copy.wait()
        field = jnp.swapaxes(held[j], 0, 1)
        south_ref[:, j] = field[:RIM]
        north_ref[:, j] = field[ROWS - RIM:]
        turned[j, :, :, :128] = field[:, :, :128]
        turned[j, :, :, 128:] = field[:, :, OWN - 128:]
    for r in range(ROWS):
        west_ref[r] = jnp.where(low_half, turned[0, r, :, :128], prev_lane(turned[1, r, :, :128], HALF))
        east_ref[r] = jnp.where(low_half, prev_lane(turned[0, r, :, 128:], HALF), turned[1, r, :, 128:])
    for r in range(ROWS // 2):
        t = r + ROWS // 2
        west_ref[ROWS + r] = jnp.where(low_half, turned[2, r, :, :128], prev_lane(turned[2, t, :, :128], HALF))
        east_ref[ROWS + r] = jnp.where(low_half, prev_lane(turned[2, r, :, 128:], HALF), turned[2, t, :, 128:])


def own_kernel(_, b_ref, x_ref, c_ref, own_ref):
    for j, ref in enumerate((b_ref, x_ref, c_ref)):
        own_ref[:, j] = jnp.swapaxes(ref[...], 0, 1)


def rim_kernel(from_east, from_west, rim_ref, north_ref, south_ref):
    low_half = lax.broadcasted_iota(jnp.int32, (LEV, 128), 1) < HALF

    for r in range(ROWS):
        east, west = from_east[r], from_west[r]
        rim_ref[r, 0] = jnp.where(low_half, east, prev_lane(west, HALF))
        rim_ref[r, 1] = jnp.where(low_half, prev_lane(east, HALF), west)
    for r in range(ROWS // 2):
        east, west = from_east[ROWS + r], from_west[ROWS + r]
        rim_ref[r, 2] = jnp.where(low_half, east, prev_lane(west, HALF))
        rim_ref[r + ROWS // 2, 2] = jnp.where(low_half, prev_lane(east, HALF), west)
    south_ref[...] = rim_ref[:RIM]
    north_ref[...] = rim_ref[ROWS - RIM:]


def restrict(m, f, e0, f1, e1, winv1, east, north, upper, even):
    i = 2 * m
    left_0 = KEEP * f[i] + around(e0, i, east, north, upper, 1)
    left_1 = KEEP * f[i + 1] + around(e0, i + 1, east, north, upper, 1)
    rhs = 0.25 * pair_sum(left_0 + left_1, even)
    f1[m] = rhs
    e1[m] = winv1 * rhs
    return left_0, left_1


def middle_left(m, f1, e1, east1, north1, upper1):
    return KEEP * f1[m] + around(e1, m, east1, north1, upper1, 2)


def hand_out(f2, e2, to_north, to_south):
    to_north[0], to_north[1] = f2[1], e2[0]
    to_south[0], to_south[1] = f2[0], e2[1]


def first_down_kernel(
    own, from_north, from_south, rim, rim_north, rim_south, sets, blocks,
    f2_out, to_north, to_south, weights2, s, e0, f1, e1, east, north, upper, winv, diag, east1, north1, upper1, winv1,
    x, lat_weight, react, react1, stage,
):
    lane = lane_ids()
    even = lane % 2 == 0
    level = lax.broadcasted_iota(jnp.int32, (LEV, LANES), 0)
    top = level == LEV - 1
    edge = top | (level == 0)
    lat = lax.axis_index("lat")
    south_end = lat == 0
    north_end = lat == lax.axis_size("lat") - 1

    def wide(column):
        return jnp.concatenate([sets[column]] * (LANES // 128), axis=1)

    def load(i, main, rims, r):
        share = jnp.concatenate([main[r, 2], rims[r, 2]], axis=1)
        s[i] = jnp.concatenate([main[r, 0], rims[r, 0]], axis=1)
        x[i] = jnp.concatenate([main[r, 1], rims[r, 1]], axis=1)
        lon_weight = wide(1) + share * wide(5)
        east[i] = 0.5 * (lon_weight + next_lane(lon_weight))
        lat_weight[i] = wide(2) + share * wide(6)
        lev_weight = wide(3) + share * wide(7)
        upper[i] = jnp.where(top, 0.0, 0.5 * (lev_weight + next_level(lev_weight)))
        react[i] = wide(0) + share * wide(4) + jnp.where(edge, 0.5 * lev_weight, 0.0)

    loop(0, RIM, lambda r: load(r, from_south, rim_south, r))
    loop(0, ROWS, lambda r: load(r + RIM, own, rim, r))
    loop(0, RIM, lambda r: load(r + RIM + ROWS, from_north, rim_north, r))

    def face(i):
        closed = (south_end & (i == RIM - 1)) | (north_end & (i == RIM + ROWS - 1))
        north[i] = jnp.where(closed, 0.0, 0.5) * (lat_weight[i] + lat_weight[i + 1])

    face(0)

    def start(i):
        face(i)
        at_end = (south_end & (i == RIM)) | (north_end & (i == RIM + ROWS - 1))
        whole = react[i] + jnp.where(at_end, 0.5, 0.0) * lat_weight[i]
        react[i] = whole
        whole = whole + east[i] + prev_lane(east[i]) + north[i] + north[i - 1]
        whole = whole + upper[i] + prev_level(upper[i])
        diag[i] = whole
        inverse = DAMP / whole
        winv[i] = inverse
        left = s[i] - (whole * x[i] - around(x, i, east, north, upper, 1))
        s[i] = left
        e0[i] = inverse * left

    loop(1, EXT - 1, start)

    north1[0] = 0.25 * pair_sum(north[1], even)

    def middle(m):
        i = 2 * m
        react1[m] = 0.25 * pair_sum(react[i] + react[i + 1], even)
        upper1[m] = 0.25 * pair_sum(upper[i] + upper[i + 1], even)
        eastern = east[i] + east[i + 1]
        east1[m] = 0.25 * jnp.where(even, next_lane(eastern), eastern)
        north1[m] = 0.25 * pair_sum(north[i + 1], even)
        whole = react1[m] + east1[m] + prev_lane(east1[m], 2) + north1[m] + north1[m - 1]
        inverse = DAMP / (whole + upper1[m] + prev_level(upper1[m]))
        winv1[m] = inverse
        restrict(m, s, e0, f1, e1, inverse, east, north, upper, even)

    loop(1, MID - 1, middle)

    last_of_four = lane % 4 == 3
    for c in range(4):
        m = 1 + 2 * c
        stage[c] = 0.125 * (react1[m] + react1[m + 1])
        stage[4 + c] = 0.125 * (upper1[m] + upper1[m + 1])
        stage[8 + c] = jnp.where(last_of_four, 0.25 * (east1[m] + east1[m + 1]), 0.0)
    for c in range(5):
        stage[12 + c] = 0.125 * north1[2 * c]
    for c in range(2):
        m = 3 + 2 * c
        left = middle_left(m, f1, e1, east1, north1, upper1)
        stage[17 + c] = 0.125 * (left + middle_left(m + 1, f1, e1, east1, north1, upper1))
    packed = times_blocks(stage[...].reshape(19 * LEV, LANES), blocks, 0).reshape(19, LEV, COLS)
    col = lax.broadcasted_iota(jnp.int32, (LEV, COLS), 1)
    empty = (col >= OWN_COLS + HALF_COLS) & (col < COLS - HALF_COLS)
    for c in range(4):
        upper2, east2, north2 = packed[4 + c], packed[8 + c], packed[13 + c]
        whole = packed[c] + east2 + prev_lane(east2) + north2 + packed[12 + c]
        whole = whole + upper2 + prev_level(upper2)
        weights2[0, 1 + c] = DAMP / jnp.where(empty, 1.0, whole)
        weights2[1, 1 + c] = east2
        weights2[2, 1 + c] = north2
        weights2[3, 1 + c] = upper2
    weights2[2, 0] = packed[12]
    f2 = (packed[17], packed[18])
    f2_out[0], f2_out[1] = f2
    hand_out(f2, (weights2[0, 2] * f2[0], weights2[0, 3] * f2[1]), to_north, to_south)


def sweep(k, f2, now, weights2):
    return KEEP * now[k] + weights2[0, k] * (
        f2[k] + around(now, k, weights2.at[1], weights2.at[2], weights2.at[3], 1)
    )


def two_sweeps(mine, north, south, weights2, f2, now, later):
    f2[1], f2[2], f2[3], f2[4] = south[0], mine[0], mine[1], north[0]
    now[0], now[5] = south[1], north[1]
    for k in range(1, 5):
        now[k] = weights2[0, k] * f2[k]
    for k in range(1, 5):
        later[k] = sweep(k, f2, now, weights2)
    return sweep(2, f2, later, weights2), sweep(3, f2, later, weights2)


def coarse_kernel(mine, from_north, from_south, weights2, f2, e2, now, later):
    e2[0], e2[1] = two_sweeps(mine, from_north, from_south, weights2, f2, now, later)


def coarse_dot_kernel(mine, from_north, from_south, weights2, sums, sum_wq, f2, e2, dots, now, later):
    e2[0], e2[1] = two_sweeps(mine, from_north, from_south, weights2, f2, now, later)
    total = jnp.zeros((LEV, OWN_COLS), F32)
    for r in range(2):
        k = 2 + r
        first = now[k]
        once, twice = later[k], e2[r]
        term = f2[k] * once + (once - first) * (twice - first) / weights2[0, k]
        total = total + term[:, :OWN_COLS]
    column = lax.broadcasted_iota(jnp.int32, dots.shape, 1)
    line = jnp.where(column == 0, jnp.sum(sums[0]), 0.0) + jnp.where(column == 1, jnp.sum(sums[1]), 0.0)
    dots[...] = line + jnp.where(column == 2, jnp.sum(sum_wq[...]) + 16.0 * jnp.sum(total), 0.0)


def ascend(
    e2, e2_north, e2_south, f2, weights2, blocks, first, end, f, e0, f1, e1, winv, east, north, upper,
    winv1, east1, north1, upper1, now, sum1, sum0, result,
):
    for r in range(2):
        now[r], now[2 + r], now[4 + r] = e2_south[r], e2[r], e2_north[r]
    rows = jnp.concatenate([sweep(k, f2, now, weights2) for k in range(1, 5)], axis=0)
    wide = times_blocks(rows, blocks, 1).reshape(4, LEV, LANES)
    for m in range(1, MID - 1):
        sum1[m] = e1[m] + wide[(m - 1) // 2]

    def middle(m):
        better = KEEP * sum1[m] + winv1[m] * (f1[m] + around(sum1, m, east1, north1, upper1, 2))
        sum0[2 * m] = e0[2 * m] + better
        sum0[2 * m + 1] = e0[2 * m + 1] + better

    loop(2, MID - 2, middle)

    def fine(i):
        result[i] = KEEP * sum0[i] + winv[i] * (f[i] + around(sum0, i, east, north, upper, 1))

    loop(first, end, fine)


def first_up_kernel(
    e2, e2_north, e2_south, f2, weights2, blocks,
    s, e0, f1, e1, winv, east, north, upper, winv1, east1, north1, upper1, diag,
    p_own, w_own, w_north, w_south, s_own, sums,
    now, sum1, sum0, p,
):
    ascend(
        e2, e2_north, e2_south, f2, weights2, blocks, RIM - 1, RIM + ROWS + 1, s, e0, f1, e1, winv, east, north, upper,
        winv1, east1, north1, upper1, now, sum1, sum0, p,
    )

    def image(r, totals):
        i = r + RIM
        w_row = diag[i] * p[i] - around(p, i, east, north, upper, 1)
        w_own[r] = w_row
        p_row, s_row = p[i, :, :OWN], s[i, :, :OWN]
        p_own[r] = p_row
        s_own[r] = s_row
        return totals[0] + s_row * p_row, totals[1] + p_row * w_row[:, :OWN]

    zero = jnp.zeros((LEV, OWN), F32)
    sums[0], sums[1] = lax.fori_loop(0, ROWS, image, (zero, zero), unroll=2)
    w_south[...] = w_own[:SEND]
    w_north[...] = w_own[ROWS - SEND:]


def second_down_kernel(
    w_own, from_north, from_south, weights2, blocks, winv, east, north, upper, winv1, east1, north1, upper1,
    f2_out, to_north, to_south, e0, f1, e1, sum_wq,
    w, stage,
):
    even = lane_ids() % 2 == 0
    w[RIM - SEND:RIM] = from_south[...]
    w[RIM + ROWS:RIM + ROWS + SEND] = from_north[...]
    for r in range(ROWS):
        w[RIM + r] = w_own[r]

    def smooth(i):
        e0[i] = winv[i] * w[i]

    loop(1, EXT - 1, smooth)

    def down(m):
        return restrict(m, w, e0, f1, e1, winv1[m], east, north, upper, even)

    loop(1, 3, down)
    loop(7, MID - 1, down)

    def down_own(m, total):
        left_0, left_1 = down(m)
        i = 2 * m
        term = e0[i] * (w[i] + left_0) + e0[i + 1] * (w[i + 1] + left_1)
        return total + term[:, :OWN]

    total = lax.fori_loop(3, 7, down_own, jnp.zeros((LEV, OWN), F32), unroll=2)
    for c in range(2):
        pair = 0.0
        for m in (3 + 2 * c, 4 + 2 * c):
            left = middle_left(m, f1, e1, east1, north1, upper1)
            total = total + 2.0 * (e1[m] * (f1[m] + left))[:, :OWN]
            pair = pair + left
        stage[c] = 0.125 * pair
    sum_wq[...] = total
    packed = times_blocks(stage[...].reshape(2 * LEV, LANES), blocks, 0).reshape(2, LEV, COLS)
    f2 = (packed[0], packed[1])
    f2_out[0], f2_out[1] = f2
    hand_out(f2, (weights2[0, 2] * f2[0], weights2[0, 3] * f2[1]), to_north, to_south)


def second_up_kernel(
    e2, e2_north, e2_south, f2, weights2, blocks,
    w_own, e0, f1, e1, winv, east, north, upper, winv1, east1, north1, upper1, dots,
    q_out, dots_out,
    now, sum1, sum0, w, result,
):
    for r in range(ROWS):
        w[RIM + r] = w_own[r]
    ascend(
        e2, e2_north, e2_south, f2, weights2, blocks, RIM, RIM + ROWS, w, e0, f1, e1, winv, east, north, upper,
        winv1, east1, north1, upper1, now, sum1, sum0, result,
    )
    dots_out[...] = dots[...]
    q_out[...] = jnp.swapaxes(result[RIM:RIM + ROWS, :, :OWN], 0, 1)


def turn_kernel(p, w, s, p_out, w_out, s_out):
    p_out[...] = jnp.swapaxes(p[...], 0, 1)
    w_out[...] = jnp.swapaxes(w[:, :, :OWN], 0, 1)
    s_out[...] = jnp.swapaxes(s[...], 0, 1)


def total_kernel(lines, total):
    total[...] = jnp.broadcast_to(jnp.sum(lines[...], axis=0, keepdims=True), total.shape)


def finish_kernel(dots, x, p, w, q, s, iterate, residual, direction):
    line = jnp.sum(dots[...], axis=0, keepdims=True)
    column = lax.broadcasted_iota(jnp.int32, (1, 128), 1)
    sp, pw, wq = [jnp.sum(jnp.where(column == j, line, 0.0), axis=1, keepdims=True)[None] for j in range(3)]
    step = sp / pw
    next_dot = (sp - step * pw) - step * (pw - step * wq)
    ratio = next_dot / sp
    iterate[...] = x[...] + step * p[...]
    residual[...] = s[...] - step * w[...]
    direction[...] = (p[...] - step * q[...]) + ratio * p[...]


def shards(right_side, initial_guess, land_mask, coefficient_sets):
    lat_size, lon_size = lax.axis_size("lat"), lax.axis_size("lon")

    def trade(to_next, to_last, axis):
        size = lax.axis_size(axis)
        up = [(i, (i + 1) % size) for i in range(size)]
        from_last = lax.ppermute(to_next, axis, up)
        return lax.ppermute(to_last, axis, [(j, i) for i, j in up]), from_last

    row, fine, mid, line = (LEV, LANES), (EXT, LEV, LANES), (MID, LEV, LANES), (LEV, COLS)
    fields = [right_side, initial_guess, land_mask]
    blocks = blocks_matrix()
    to_north, to_south, to_east, to_west = call(
        pack_kernel,
        [(RIM, 3, LEV, OWN)] * 2 + [(12, LEV, 128)] * 2,
        fields,
        [(3, LEV, ROWS, OWN), (3, ROWS, LEV, 256)],
        specs=[HBM] * 3,
        copies=3,
    )
    lat_rows = trade(to_north, to_south, "lat")
    lon_rims = trade(to_east, to_west, "lon")
    (own,) = call(own_kernel, [(ROWS, 3, LEV, OWN)], [to_west] + fields, specs=[HBM])
    rim, to_north, to_south = call(
        rim_kernel, [(ROWS, 3, LEV, 128), (RIM, 3, LEV, 128), (RIM, 3, LEV, 128)], lon_rims
    )
    lat_rims = trade(to_north, to_south, "lat")
    sea, land = coefficient_sets[0], coefficient_sets[1]
    sets = jnp.broadcast_to(jnp.concatenate([sea, land - sea])[:, :, None], (8, LEV, 128))

    (f2, to_north, to_south, weights2, s, e0, f1, e1, east, north, upper, winv, diag, east1, north1, upper1, winv1) = call(
        first_down_kernel,
        [(2,) + line] * 3 + [(4, NEAR) + line, fine, fine, mid, mid, fine, fine, fine, fine, fine, mid, mid, mid, mid],
        [own, *lat_rows, rim, *lat_rims, sets, blocks],
        [fine, fine, fine, mid, (19,) + row],
    )
    grids = [winv, east, north, upper, winv1, east1, north1, upper1]
    near = (NEAR,) + line
    f2_near, e2 = call(
        coarse_kernel, [near, (2,) + line], [f2, *trade(to_north, to_south, "lat"), weights2], [near, near]
    )
    p_own, w_own, to_north, to_south, s_own, sums = call(
        first_up_kernel,
        [(ROWS, LEV, OWN), (ROWS,) + row, (SEND,) + row, (SEND,) + row, (ROWS, LEV, OWN), (2, LEV, OWN)],
        [e2, *trade(e2, e2, "lat"), f2_near, weights2, blocks, s, e0, f1, e1] + grids + [diag],
        [near, mid, fine, fine],
    )
    w_rows = trade(to_north, to_south, "lat")
    p, w, s = call(turn_kernel, [(LEV, ROWS, OWN)] * 3, [p_own, w_own, s_own])
    f2, to_north, to_south, e0, f1, e1, sum_wq = call(
        second_down_kernel,
        [(2,) + line] * 3 + [fine, mid, mid, (LEV, OWN)],
        [w_own, *w_rows, weights2, blocks] + grids,
        [fine, (2,) + row],
    )
    f2_near, e2, dots = call(
        coarse_dot_kernel,
        [near, (2,) + line, (lon_size, 128)],
        [f2, *trade(to_north, to_south, "lat"), weights2, sums, sum_wq],
        [near, near],
    )
    q, dots = call(
        second_up_kernel,
        [(LEV, ROWS, OWN), (lon_size, 128)],
        [e2, *trade(e2, e2, "lat"), f2_near, weights2, blocks, w_own, e0, f1, e1] + grids + [dots],
        [near, mid, fine, fine, fine],
    )
    (dots,) = call(total_kernel, [(lat_size, 128)], [lax.all_to_all(dots, "lon", 0, 0, tiled=True)])
    dots = lax.all_to_all(dots, "lat", 0, 0, tiled=True)
    return tuple(call(finish_kernel, [(LEV, ROWS, OWN)] * 3, [dots, initial_guess, p, w, q, s]))


def solution(mesh):
    field = P(None, "lat", "lon")
    return jax.shard_map(
        shards, mesh=mesh, in_specs=(field, field, field, P()), out_specs=(field, field, field), check_vma=False
    )
```

```python
import jax
import jax.numpy as jnp
import numpy as np
from jax import lax
from jax.experimental import pallas as pl
from jax.experimental.pallas import tpu as pltpu
from jax.sharding import PartitionSpec as P


LEV = 16
ROWS = 8
OWN = 512
HALF = 64
DEEP = 42
LANES = OWN + 2 * HALF
RIM = 6
EXT = ROWS + 2 * RIM
MID = EXT // 2
SEND = 5
NEAR = 6
COLS = 256
OWN_COLS = OWN // 4
HALF_COLS = HALF // 4
DAMP = 0.8
KEEP = 1.0 - DAMP
F32 = jnp.float32

VMEM = pl.BlockSpec(memory_space=pltpu.VMEM)
HBM = pl.BlockSpec(memory_space=pltpu.HBM)


def call(body, outs, ins, scratch=(), specs=(), copies=0):
    return pl.pallas_call(
        body,
        out_shape=[jax.ShapeDtypeStruct(o, F32) for o in outs],
        in_specs=list(specs) + [VMEM] * (len(ins) - len(specs)),
        out_specs=[VMEM] * len(outs),
        scratch_shapes=[pltpu.VMEM(s, F32) for s in scratch] + [pltpu.SemaphoreType.DMA((copies,))] * (copies > 0),
        compiler_params=pltpu.CompilerParams(vmem_limit_bytes=(60 if copies else 24) * 1024 * 1024),
        cost_estimate=pl.CostEstimate(flops=1000000, bytes_accessed=1000000, transcendentals=0),
    )(*ins)


def loop(first, end, body, unroll=3):
    def step(i, carry):
        body(i)
        return carry

    lax.fori_loop(first, end, step, 0, unroll=unroll)


def lane_ids():
    return lax.broadcasted_iota(jnp.int32, (LEV, LANES), 1)


def next_lane(v, n=1):
    return pltpu.roll(v, v.shape[-1] - n, axis=1)


def prev_lane(v, n=1):
    return pltpu.roll(v, n, axis=1)


def next_level(v):
    return pltpu.roll(v, LEV - 1, axis=0)


def prev_level(v):
    return pltpu.roll(v, 1, axis=0)


def pair_sum(v, even):
    return v + jnp.where(even, next_lane(v), prev_lane(v))


def around(v, i, east, north, upper, n):
    here = v[i]
    total = east[i] * next_lane(here, n) + prev_lane(east[i] * here, n)
    total = total + upper[i] * next_level(here) + prev_level(upper[i] * here)
    return total + north[i] * v[i + 1] + north[i - 1] * v[i - 1]


def blocks_matrix():
    lane = np.arange(LANES)
    cell = lane // 4
    cell = np.where(cell < OWN_COLS + HALF_COLS, cell, cell + COLS - LANES // 4)
    matrix = np.zeros((LANES, COLS), np.float32)
    matrix[lane, cell] = 1.0
    return jnp.asarray(matrix, jnp.bfloat16)


def times_blocks(rows, blocks, side):
    total = 0.0
    left = rows
    for _ in range(3):
        part = left.astype(jnp.bfloat16)
        left = left - part.astype(F32)
        total = total + lax.dot_general(part, blocks[...], (((1,), (side,)), ((), ())), preferred_element_type=F32)
    return total


def pack_kernel(b_ref, x_ref, c_ref, north_ref, south_ref, east_ref, west_ref, held, turned, arrived):
    lane = lax.broadcasted_iota(jnp.int32, (LEV, 128), 1)
    copies = [pltpu.make_async_copy(ref, held.at[j], arrived.at[j]) for j, ref in enumerate((b_ref, x_ref, c_ref))]
    for copy in copies:
        copy.start()
    for j, copy in enumerate(copies):
        copy.wait()
        field = jnp.swapaxes(held[j], 0, 1)
        south_ref[:, j] = field[:RIM]
        north_ref[:, j] = field[ROWS - RIM:]
        turned[j, :, :, :128] = field[:, :, :128]
        turned[j, :, :, 128:] = field[:, :, OWN - 128:]
    for r in range(ROWS):
        b, x, c = [turned[j, r, :, :128] for j in range(3)]
        west_ref[r] = jnp.where(lane < DEEP, b, jnp.where(lane < 2 * DEEP, prev_lane(x, DEEP), prev_lane(c, 2 * DEEP)))
        b, x, c = [turned[j, r, :, 128:] for j in range(3)]
        x, c = next_lane(x, DEEP), next_lane(c, 2 * DEEP)
        east_ref[r] = jnp.where(lane >= 128 - DEEP, b, jnp.where(lane >= 128 - 2 * DEEP, x, c))


def rim_kernel(from_east, from_west, rim_ref, north_ref, south_ref):
    lane = lax.broadcasted_iota(jnp.int32, (LEV, 128), 1)
    for r in range(ROWS):
        east, west = from_east[r], from_west[r]
        for j in range(3):
            if j > 0:
                east, west = next_lane(east, DEEP), prev_lane(west, DEEP)
            rim_ref[r, j] = jnp.where(lane < DEEP, east, jnp.where(lane >= 128 - DEEP, west, 0.0))
    south_ref[...] = rim_ref[:RIM]
    north_ref[...] = rim_ref[ROWS - RIM:]


def restrict(m, f, e0, f1, e1, winv1, east, north, upper, even):
    i = 2 * m
    left_0 = KEEP * f[i] + around(e0, i, east, north, upper, 1)
    left_1 = KEEP * f[i + 1] + around(e0, i + 1, east, north, upper, 1)
    rhs = 0.25 * pair_sum(left_0 + left_1, even)
    f1[m] = rhs
    e1[m] = winv1 * rhs
    return left_0, left_1


def middle_left(m, f1, e1, east1, north1, upper1):
    return KEEP * f1[m] + around(e1, m, east1, north1, upper1, 2)


def hand_out(f2, e2, to_north, to_south):
    to_north[0], to_north[1] = f2[1], e2[0]
    to_south[0], to_south[1] = f2[0], e2[1]


def weigh(sets, share, width):
    level = lax.broadcasted_iota(jnp.int32, (LEV, width), 0)
    top = level == LEV - 1
    edge = top | (level == 0)

    def blend(column):
        sea = jnp.concatenate([sets[column]] * (width // 128), axis=1)
        return sea + share * jnp.concatenate([sets[column + 4]] * (width // 128), axis=1)

    lev_weight = blend(3)
    react = blend(0) + jnp.where(edge, 0.5 * lev_weight, 0.0)
    upper = jnp.where(top, 0.0, 0.5 * (lev_weight + next_level(lev_weight)))
    return react, upper, blend(1), blend(2)


def weigh_kernel(
    b_ref, x_ref, c_ref, from_north, from_south, sets,
    b, x, react, upper, lon_weight, lat_weight,
    share,
):
    share[...] = jnp.swapaxes(c_ref[...], 0, 1)
    b[RIM:RIM + ROWS] = jnp.swapaxes(b_ref[...], 0, 1)
    x[RIM:RIM + ROWS] = jnp.swapaxes(x_ref[...], 0, 1)

    def own(r):
        i = r + RIM
        react[i], upper[i], lon_weight[i], lat_weight[i] = weigh(sets, share[r], OWN)

    def outer(i, rows, r):
        b[i] = rows[r, 0]
        x[i] = rows[r, 1]
        react[i], upper[i], lon_weight[i], lat_weight[i] = weigh(sets, rows[r, 2], OWN)

    loop(0, ROWS, own)
    loop(0, RIM, lambda r: outer(r, from_south, r))
    loop(0, RIM, lambda r: outer(r + RIM + ROWS, from_north, r))


class Joined:
    def __init__(self, main, rims):
        self.main, self.rims = main, rims

    def __getitem__(self, i):
        return jnp.concatenate([self.main[i], self.rims[i]], axis=1)


def first_down_kernel(
    b_main, x_main, react_main, upper_main, lon_main, lat_main, rim, rim_north, rim_south, sets, blocks,
    s, f2_out, to_north, to_south, weights2, e0, f1, e1, east, north, upper, winv, diag, east1, north1, upper1, winv1,
    b_rims, x_rims, react_rims, upper_rims, lon_rims, lat_rims, react, react1, stage,
):
    b, x, react_in = Joined(b_main, b_rims), Joined(x_main, x_rims), Joined(react_main, react_rims)
    upper_in, lon_weight, lat_weight = Joined(upper_main, upper_rims), Joined(lon_main, lon_rims), Joined(lat_main, lat_rims)
    lane = lane_ids()
    even = lane % 2 == 0
    lat = lax.axis_index("lat")
    south_end = lat == 0
    north_end = lat == lax.axis_size("lat") - 1

    def take(i, rows, r):
        b_rims[i] = rows[r, 0]
        x_rims[i] = rows[r, 1]
        react_rims[i], upper_rims[i], lon_rims[i], lat_rims[i] = weigh(sets, rows[r, 2], 128)

    for r in range(RIM):
        take(r, rim_south, r)
        take(r + RIM + ROWS, rim_north, r)
    for r in range(ROWS):
        take(r + RIM, rim, r)

    def face_east(i):
        here = lon_weight[i]
        east[i] = 0.5 * (here + next_lane(here))
        upper[i] = upper_in[i]

    face_east(0)
    face_east(EXT - 1)

    def face(i):
        closed = (south_end & (i == RIM - 1)) | (north_end & (i == RIM + ROWS - 1))
        north[i] = jnp.where(closed, 0.0, 0.5) * (lat_weight[i] + lat_weight[i + 1])

    face(0)

    def start(i):
        face(i)
        face_east(i)
        at_end = (south_end & (i == RIM)) | (north_end & (i == RIM + ROWS - 1))
        whole = react_in[i] + jnp.where(at_end, 0.5, 0.0) * lat_weight[i]
        react[i] = whole
        whole = whole + east[i] + prev_lane(east[i]) + north[i] + north[i - 1]
        whole = whole + upper[i] + prev_level(upper[i])
        diag[i] = whole
        inverse = DAMP / whole
        winv[i] = inverse
        left = b[i] - (whole * x[i] - around(x, i, east, north, upper, 1))
        s[i] = left
        e0[i] = inverse * left

    loop(1, EXT - 1, start)

    north1[0] = 0.25 * pair_sum(north[1], even)

    def middle(m):
        i = 2 * m
        react1[m] = 0.25 * pair_sum(react[i] + react[i + 1], even)
        upper1[m] = 0.25 * pair_sum(upper[i] + upper[i + 1], even)
        eastern = east[i] + east[i + 1]
        east1[m] = 0.25 * jnp.where(even, next_lane(eastern), eastern)
        north1[m] = 0.25 * pair_sum(north[i + 1], even)
        whole = react1[m] + east1[m] + prev_lane(east1[m], 2) + north1[m] + north1[m - 1]
        inverse = DAMP / (whole + upper1[m] + prev_level(upper1[m]))
        winv1[m] = inverse
        restrict(m, s, e0, f1, e1, inverse, east, north, upper, even)

    loop(1, MID - 1, middle)

    last_of_four = lane % 4 == 3
    for c in range(4):
        m = 1 + 2 * c
        stage[c] = 0.125 * (react1[m] + react1[m + 1])
        stage[4 + c] = 0.125 * (upper1[m] + upper1[m + 1])
        stage[8 + c] = jnp.where(last_of_four, 0.25 * (east1[m] + east1[m + 1]), 0.0)
    for c in range(5):
        stage[12 + c] = 0.125 * north1[2 * c]
    for c in range(2):
        m = 3 + 2 * c
        left = middle_left(m, f1, e1, east1, north1, upper1)
        stage[17 + c] = 0.125 * (left + middle_left(m + 1, f1, e1, east1, north1, upper1))
    packed = times_blocks(stage[...].reshape(19 * LEV, LANES), blocks, 0).reshape(19, LEV, COLS)
    col = lax.broadcasted_iota(jnp.int32, (LEV, COLS), 1)
    empty = (col >= OWN_COLS + HALF_COLS) & (col < COLS - HALF_COLS)
    for c in range(4):
        upper2, east2, north2 = packed[4 + c], packed[8 + c], packed[13 + c]
        whole = packed[c] + east2 + prev_lane(east2) + north2 + packed[12 + c]
        whole = whole + upper2 + prev_level(upper2)
        weights2[0, 1 + c] = DAMP / jnp.where(empty, 1.0, whole)
        weights2[1, 1 + c] = east2
        weights2[2, 1 + c] = north2
        weights2[3, 1 + c] = upper2
    weights2[2, 0] = packed[12]
    f2 = (packed[17], packed[18])
    f2_out[0], f2_out[1] = f2
    hand_out(f2, (weights2[0, 2] * f2[0], weights2[0, 3] * f2[1]), to_north, to_south)


def sweep(k, f2, now, weights2):
    return KEEP * now[k] + weights2[0, k] * (
        f2[k] + around(now, k, weights2.at[1], weights2.at[2], weights2.at[3], 1)
    )


def two_sweeps(mine, north, south, weights2, f2, now, later):
    f2[1], f2[2], f2[3], f2[4] = south[0], mine[0], mine[1], north[0]
    now[0], now[5] = south[1], north[1]
    for k in range(1, 5):
        now[k] = weights2[0, k] * f2[k]
    for k in range(1, 5):
        later[k] = sweep(k, f2, now, weights2)
    return sweep(2, f2, later, weights2), sweep(3, f2, later, weights2)


def coarse_kernel(mine, from_north, from_south, weights2, f2, e2, e2_again, now, later):
    e2[0], e2[1] = two_sweeps(mine, from_north, from_south, weights2, f2, now, later)
    e2_again[...] = e2[...]


def coarse_dot_kernel(mine, from_north, from_south, weights2, sums, sum_wq, f2, e2, e2_again, dots, now, later):
    e2[0], e2[1] = two_sweeps(mine, from_north, from_south, weights2, f2, now, later)
    e2_again[...] = e2[...]
    total = jnp.zeros((LEV, OWN_COLS), F32)
    for r in range(2):
        k = 2 + r
        first = now[k]
        once, twice = later[k], e2[r]
        term = f2[k] * once + (once - first) * (twice - first) / weights2[0, k]
        total = total + term[:, :OWN_COLS]
    column = lax.broadcasted_iota(jnp.int32, dots.shape, 1)
    line = jnp.where(column == 0, jnp.sum(sums[0]), 0.0) + jnp.where(column == 1, jnp.sum(sums[1]), 0.0)
    dots[...] = line + jnp.where(column == 2, jnp.sum(sum_wq[...]) + 16.0 * jnp.sum(total), 0.0)


def ascend(
    e2, e2_north, e2_south, f2, weights2, blocks, first, end, f, e0, f1, e1, winv, east, north, upper,
    winv1, east1, north1, upper1, now, sum1, sum0, result,
):
    for r in range(2):
        now[r], now[2 + r], now[4 + r] = e2_south[r], e2[r], e2_north[r]
    rows = jnp.concatenate([sweep(k, f2, now, weights2) for k in range(1, 5)], axis=0)
    wide = times_blocks(rows, blocks, 1).reshape(4, LEV, LANES)
    for m in range(1, MID - 1):
        sum1[m] = e1[m] + wide[(m - 1) // 2]

    def middle(m):
        better = KEEP * sum1[m] + winv1[m] * (f1[m] + around(sum1, m, east1, north1, upper1, 2))
        sum0[2 * m] = e0[2 * m] + better
        sum0[2 * m + 1] = e0[2 * m + 1] + better

    loop(2, MID - 2, middle)

    def fine(i):
        result[i] = KEEP * sum0[i] + winv[i] * (f[i] + around(sum0, i, east, north, upper, 1))

    loop(first, end, fine)


def first_up_kernel(
    e2, e2_north, e2_south, f2, weights2, blocks,
    s, e0, f1, e1, winv, east, north, upper, winv1, east1, north1, upper1, diag,
    p_own, w_own, w_north, w_south, s_own, sums,
    now, sum1, sum0, p,
):
    ascend(
        e2, e2_north, e2_south, f2, weights2, blocks, RIM - 1, RIM + ROWS + 1, s, e0, f1, e1, winv, east, north, upper,
        winv1, east1, north1, upper1, now, sum1, sum0, p,
    )

    def image(r, totals):
        i = r + RIM
        w_row = diag[i] * p[i] - around(p, i, east, north, upper, 1)
        w_own[r] = w_row
        p_row, s_row = p[i, :, :OWN], s[i, :, :OWN]
        p_own[r] = p_row
        s_own[r] = s_row
        return totals[0] + s_row * p_row, totals[1] + p_row * w_row[:, :OWN]

    zero = jnp.zeros((LEV, OWN), F32)
    sums[0], sums[1] = lax.fori_loop(0, ROWS, image, (zero, zero), unroll=2)
    w_south[...] = w_own[:SEND]
    w_north[...] = w_own[ROWS - SEND:]


def second_down_kernel(
    w_own, from_north, from_south, weights2, blocks, winv, east, north, upper, winv1, east1, north1, upper1,
    f2_out, to_north, to_south, e0, f1, e1, sum_wq,
    w, stage,
):
    even = lane_ids() % 2 == 0
    w[RIM - SEND:RIM] = from_south[...]
    w[RIM + ROWS:RIM + ROWS + SEND] = from_north[...]
    for r in range(ROWS):
        w[RIM + r] = w_own[r]

    def smooth(i):
        e0[i] = winv[i] * w[i]

    loop(1, EXT - 1, smooth)

    def down(m):
        return restrict(m, w, e0, f1, e1, winv1[m], east, north, upper, even)

    loop(1, 3, down, 2)
    loop(7, MID - 1, down, 2)

    def down_own(m, total):
        left_0, left_1 = down(m)
        i = 2 * m
        term = e0[i] * (w[i] + left_0) + e0[i + 1] * (w[i + 1] + left_1)
        return total + term[:, :OWN]

    total = lax.fori_loop(3, 7, down_own, jnp.zeros((LEV, OWN), F32), unroll=2)
    for c in range(2):
        pair = 0.0
        for m in (3 + 2 * c, 4 + 2 * c):
            left = middle_left(m, f1, e1, east1, north1, upper1)
            total = total + 2.0 * (e1[m] * (f1[m] + left))[:, :OWN]
            pair = pair + left
        stage[c] = 0.125 * pair
    sum_wq[...] = total
    packed = times_blocks(stage[...].reshape(2 * LEV, LANES), blocks, 0).reshape(2, LEV, COLS)
    f2 = (packed[0], packed[1])
    f2_out[0], f2_out[1] = f2
    hand_out(f2, (weights2[0, 2] * f2[0], weights2[0, 3] * f2[1]), to_north, to_south)


def second_up_kernel(
    e2, e2_north, e2_south, f2, weights2, blocks,
    w_own, e0, f1, e1, winv, east, north, upper, winv1, east1, north1, upper1, dots,
    q_out, dots_out,
    now, sum1, sum0, w, result,
):
    for r in range(ROWS):
        w[RIM + r] = w_own[r]
    ascend(
        e2, e2_north, e2_south, f2, weights2, blocks, RIM, RIM + ROWS, w, e0, f1, e1, winv, east, north, upper,
        winv1, east1, north1, upper1, now, sum1, sum0, result,
    )
    dots_out[...] = dots[...]
    q_out[...] = jnp.swapaxes(result[RIM:RIM + ROWS, :, :OWN], 0, 1)


def turn_kernel(p, w, s, p_out, w_out, s_out):
    p_out[...] = jnp.swapaxes(p[...], 0, 1)
    w_out[...] = jnp.swapaxes(w[:, :, :OWN], 0, 1)
    s_out[...] = jnp.swapaxes(s[...], 0, 1)


def total_kernel(lines, total):
    total[...] = jnp.broadcast_to(jnp.sum(lines[...], axis=0, keepdims=True), total.shape)


def finish_kernel(dots, x, p, w, q, s, iterate, residual, direction):
    line = jnp.sum(dots[...], axis=0, keepdims=True)
    column = lax.broadcasted_iota(jnp.int32, (1, 128), 1)
    sp, pw, wq = [jnp.sum(jnp.where(column == j, line, 0.0), axis=1, keepdims=True)[None] for j in range(3)]
    step = sp / pw
    next_dot = (sp - step * pw) - step * (pw - step * wq)
    ratio = next_dot / sp
    iterate[...] = x[...] + step * p[...]
    residual[...] = s[...] - step * w[...]
    direction[...] = (p[...] - step * q[...]) + ratio * p[...]


def shards(right_side, initial_guess, land_mask, coefficient_sets):
    z_size, lat_size = lax.axis_size("z"), lax.axis_size("lat")
    lines = (lax.axis_size("x") * lat_size, 128)
    lon = ("x", "z")
    sizes = {lon: lax.axis_size("x") * z_size, "lat": lat_size}

    def trade(to_next, to_last, axis):
        size = sizes[axis]
        up = [(i, (i + 1) % size) for i in range(size)]
        from_last = lax.ppermute(to_next, axis, up)
        return lax.ppermute(to_last, axis, [(j, i) for i, j in up]), from_last

    row, fine, mid, line = (LEV, LANES), (EXT, LEV, LANES), (MID, LEV, LANES), (LEV, COLS)
    fields = [right_side, initial_guess, land_mask]
    blocks = blocks_matrix()
    to_north, to_south, to_east, to_west = call(
        pack_kernel,
        [(RIM, 3, LEV, OWN)] * 2 + [(ROWS, LEV, 128)] * 2,
        fields,
        [(3, LEV, ROWS, OWN), (3, ROWS, LEV, 256)],
        specs=[HBM] * 3,
        copies=3,
    )
    lat_rows = trade(to_north, to_south, "lat")
    lon_rims = trade(to_east, to_west, lon)
    rim, to_north, to_south = call(
        rim_kernel, [(ROWS, 3, LEV, 128), (RIM, 3, LEV, 128), (RIM, 3, LEV, 128)], lon_rims
    )
    lat_rims = trade(to_north, to_south, "lat")
    sea, land = coefficient_sets[0], coefficient_sets[1]
    sets = jnp.broadcast_to(jnp.concatenate([sea, land - sea])[:, :, None], (8, LEV, 128))

    main, side = (EXT, LEV, OWN), (EXT, LEV, 128)
    weighed = call(weigh_kernel, [main] * 6, fields + [*lat_rows, sets], [(ROWS, LEV, OWN)])
    (s, f2, to_north, to_south, weights2, e0, f1, e1, east, north, upper, winv, diag, east1, north1, upper1, winv1) = call(
        first_down_kernel,
        [fine] + [(2,) + line] * 3 + [(4, NEAR) + line, fine, mid, mid, fine, fine, fine, fine, fine, mid, mid, mid, mid],
        [*weighed, rim, *lat_rims, sets, blocks],
        [side] * 6 + [fine, mid, (19,) + row],
    )
    grids = [winv, east, north, upper, winv1, east1, north1, upper1]
    near = (NEAR,) + line
    f2_near, e2, e2_again = call(
        coarse_kernel,
        [near, (2,) + line, (2,) + line],
        [f2, *trade(to_north, to_south, "lat"), weights2],
        [near, near],
    )
    p_own, w_own, to_north, to_south, s_own, sums = call(
        first_up_kernel,
        [(ROWS, LEV, OWN), (ROWS,) + row, (SEND,) + row, (SEND,) + row, (ROWS, LEV, OWN), (2, LEV, OWN)],
        [e2, *trade(e2, e2_again, "lat"), f2_near, weights2, blocks, s, e0, f1, e1] + grids + [diag],
        [near, mid, fine, fine],
    )
    w_rows = trade(to_north, to_south, "lat")
    p, w, s = call(turn_kernel, [(LEV, ROWS, OWN)] * 3, [p_own, w_own, s_own])
    f2, to_north, to_south, e0, f1, e1, sum_wq = call(
        second_down_kernel,
        [(2,) + line] * 3 + [fine, mid, mid, (LEV, OWN)],
        [w_own, *w_rows, weights2, blocks] + grids,
        [fine, (2,) + row],
    )
    f2_near, e2, e2_again, dots = call(
        coarse_dot_kernel,
        [near, (2,) + line, (2,) + line, lines],
        [f2, *trade(to_north, to_south, "lat"), weights2, sums, sum_wq],
        [near, near],
    )
    q, dots = call(
        second_up_kernel,
        [(LEV, ROWS, OWN), lines],
        [e2, *trade(e2, e2_again, "lat"), f2_near, weights2, blocks, w_own, e0, f1, e1] + grids + [dots],
        [near, mid, fine, fine, fine],
    )
    (dots,) = call(total_kernel, [(z_size, 128)], [lax.all_to_all(dots, ("x", "lat"), 0, 0, tiled=True)])
    dots = lax.all_to_all(dots, "z", 0, 0, tiled=True)
    return tuple(call(finish_kernel, [(LEV, ROWS, OWN)] * 3, [dots, initial_guess, p, w, q, s]))


def solution(mesh):
    lon, lat = mesh.shape["lon"], mesh.shape["lat"]
    z = 16 if lon % 16 == 0 else lon
    grid = jax.sharding.Mesh(mesh.devices.reshape(lon // z, z, lat), ("x", "z", "lat"))
    field = P(None, "lat", ("x", "z"))
    return jax.shard_map(
        shards, mesh=grid, in_specs=(field, field, field, P()), out_specs=(field, field, field), check_vma=False
    )
```

```python
import jax
import jax.numpy as jnp
import numpy as np
from jax import lax
from jax.experimental import pallas as pl
from jax.experimental.pallas import tpu as pltpu
from jax.sharding import PartitionSpec as P


LEV = 16
ROWS = 8
OWN = 512
HALF = 64
DEEP = 42
LANES = OWN + 2 * HALF
RIM = 4
EXT = ROWS + 2 * RIM
MID = EXT // 2
SEND = 3
NEAR = 6
COLS = 256
OWN_COLS = OWN // 4
HALF_COLS = HALF // 4
DAMP = 0.8
KEEP = 1.0 - DAMP
F32 = jnp.float32

VMEM = pl.BlockSpec(memory_space=pltpu.VMEM)
HBM = pl.BlockSpec(memory_space=pltpu.HBM)


def call(body, outs, ins, scratch=(), specs=(), copies=0):
    return pl.pallas_call(
        body,
        out_shape=[jax.ShapeDtypeStruct(o, F32) for o in outs],
        in_specs=list(specs) + [VMEM] * (len(ins) - len(specs)),
        out_specs=[VMEM] * len(outs),
        scratch_shapes=[pltpu.VMEM(s, F32) for s in scratch] + [pltpu.SemaphoreType.DMA((copies,))] * (copies > 0),
        compiler_params=pltpu.CompilerParams(vmem_limit_bytes=(60 if copies else 24) * 1024 * 1024),
        cost_estimate=pl.CostEstimate(flops=1000000, bytes_accessed=1000000, transcendentals=0),
    )(*ins)


def loop(first, end, body):
    rows = end - first

    def step(i, carry):
        body(i)
        return carry

    lax.fori_loop(first, end, step, 0, unroll=rows if rows <= 8 else rows // 2)


def lane_ids():
    return lax.broadcasted_iota(jnp.int32, (LEV, LANES), 1)


def next_lane(v, n=1):
    return pltpu.roll(v, v.shape[-1] - n, axis=1)


def prev_lane(v, n=1):
    return pltpu.roll(v, n, axis=1)


def next_level(v):
    return pltpu.roll(v, LEV - 1, axis=0)


def prev_level(v):
    return pltpu.roll(v, 1, axis=0)


def pair_sum(v, even):
    return v + jnp.where(even, next_lane(v), prev_lane(v))


def around(v, i, east, north, upper, n):
    here = v[i]
    total = east[i] * next_lane(here, n) + prev_lane(east[i] * here, n)
    total = total + upper[i] * next_level(here) + prev_level(upper[i] * here)
    return total + north[i] * v[i + 1] + north[i - 1] * v[i - 1]


def blocks_matrix():
    lane = np.arange(LANES)
    cell = lane // 4
    cell = np.where(cell < OWN_COLS + HALF_COLS, cell, cell + COLS - LANES // 4)
    matrix = np.zeros((LANES, COLS), np.float32)
    matrix[lane, cell] = 1.0
    return jnp.asarray(matrix, jnp.bfloat16)


def times_blocks(rows, blocks, side):
    total = 0.0
    left = rows
    for _ in range(3):
        part = left.astype(jnp.bfloat16)
        left = left - part.astype(F32)
        total = total + lax.dot_general(part, blocks[...], (((1,), (side,)), ((), ())), preferred_element_type=F32)
    return total


def pack_kernel(b_ref, x_ref, c_ref, north_ref, south_ref, east_ref, west_ref, held, turned, arrived):
    lane = lax.broadcasted_iota(jnp.int32, (LEV, 128), 1)
    copies = [pltpu.make_async_copy(ref, held.at[j], arrived.at[j]) for j, ref in enumerate((b_ref, x_ref, c_ref))]
    for copy in copies:
        copy.start()
    for j, copy in enumerate(copies):
        copy.wait()
        field = jnp.swapaxes(held[j], 0, 1)
        south_ref[:, j] = field[:RIM]
        north_ref[:, j] = field[ROWS - RIM:]
        turned[j, :, :, :128] = field[:, :, :128]
        turned[j, :, :, 128:] = field[:, :, OWN - 128:]
    for r in range(ROWS):
        b, x, c = [turned[j, r, :, :128] for j in range(3)]
        west_ref[r] = jnp.where(lane < DEEP, b, jnp.where(lane < 2 * DEEP, prev_lane(x, DEEP), prev_lane(c, 2 * DEEP)))
        b, x, c = [turned[j, r, :, 128:] for j in range(3)]
        x, c = next_lane(x, DEEP), next_lane(c, 2 * DEEP)
        east_ref[r] = jnp.where(lane >= 128 - DEEP, b, jnp.where(lane >= 128 - 2 * DEEP, x, c))


def rim_kernel(from_east, from_west, rim_ref, north_ref, south_ref):
    lane = lax.broadcasted_iota(jnp.int32, (LEV, 128), 1)
    for r in range(ROWS):
        east, west = from_east[r], from_west[r]
        for j in range(3):
            if j > 0:
                east, west = next_lane(east, DEEP), prev_lane(west, DEEP)
            rim_ref[r, j] = jnp.where(lane < DEEP, east, jnp.where(lane >= 128 - DEEP, west, 0.0))
    south_ref[...] = rim_ref[:RIM]
    north_ref[...] = rim_ref[ROWS - RIM:]


def restrict(m, f, e0, f1, e1, winv1, east, north, upper, even):
    i = 2 * m
    left_0 = KEEP * f[i] + around(e0, i, east, north, upper, 1)
    left_1 = KEEP * f[i + 1] + around(e0, i + 1, east, north, upper, 1)
    rhs = 0.25 * pair_sum(left_0 + left_1, even)
    f1[m] = rhs
    e1[m] = winv1 * rhs
    return left_0, left_1


def middle_left(m, f1, e1, east1, north1, upper1):
    return KEEP * f1[m] + around(e1, m, east1, north1, upper1, 2)


def hand_out(f2, e2, weights2, to_north, to_south):
    to_north[0], to_north[1] = f2[1], e2[0]
    to_south[0], to_south[1] = f2[0], e2[1]
    if to_north.shape[0] > 2:
        for j, kind in enumerate((0, 1, 3)):
            to_north[2 + j] = weights2[kind, 3]
            to_south[2 + j] = weights2[kind, 2]
        to_north[5] = weights2[2, 2]
        to_south[5] = weights2[2, 2]


def weigh(sets, share, width):
    level = lax.broadcasted_iota(jnp.int32, (LEV, width), 0)
    top = level == LEV - 1
    edge = top | (level == 0)

    def blend(column):
        sea = jnp.concatenate([sets[column]] * (width // 128), axis=1)
        return sea + share * jnp.concatenate([sets[column + 4]] * (width // 128), axis=1)

    lev_weight = blend(3)
    react = blend(0) + jnp.where(edge, 0.5 * lev_weight, 0.0)
    upper = jnp.where(top, 0.0, 0.5 * (lev_weight + next_level(lev_weight)))
    return react, upper, blend(1), blend(2)


def weigh_kernel(
    b_ref, x_ref, c_ref, from_north, from_south, sets,
    b, x, react, upper, lon_weight, lat_weight,
    share,
):
    share[...] = jnp.swapaxes(c_ref[...], 0, 1)
    b[RIM:RIM + ROWS] = jnp.swapaxes(b_ref[...], 0, 1)
    x[RIM:RIM + ROWS] = jnp.swapaxes(x_ref[...], 0, 1)

    def own(r):
        i = r + RIM
        react[i], upper[i], lon_weight[i], lat_weight[i] = weigh(sets, share[r], OWN)

    def outer(i, rows, r):
        b[i] = rows[r, 0]
        x[i] = rows[r, 1]
        react[i], upper[i], lon_weight[i], lat_weight[i] = weigh(sets, rows[r, 2], OWN)

    loop(0, ROWS, own)
    loop(0, RIM, lambda r: outer(r, from_south, r))
    loop(0, RIM, lambda r: outer(r + RIM + ROWS, from_north, r))


class Joined:
    def __init__(self, main, rims):
        self.main, self.rims = main, rims

    def __getitem__(self, i):
        return jnp.concatenate([self.main[i], self.rims[i]], axis=1)


def first_down_kernel(
    b_main, x_main, react_main, upper_main, lon_main, lat_main, rim, rim_north, rim_south, sets, blocks,
    s, f2_out, to_north, to_south, weights2, e0, f1, e1, east, north, upper, winv, diag, east1, north1, upper1, winv1,
    b_rims, x_rims, react_rims, upper_rims, lon_rims, lat_rims, react, react1, stage,
):
    b, x, react_in = Joined(b_main, b_rims), Joined(x_main, x_rims), Joined(react_main, react_rims)
    upper_in, lon_weight, lat_weight = Joined(upper_main, upper_rims), Joined(lon_main, lon_rims), Joined(lat_main, lat_rims)
    lane = lane_ids()
    even = lane % 2 == 0
    lat = lax.axis_index("lat")
    south_end = lat == 0
    north_end = lat == lax.axis_size("lat") - 1

    def take(i, rows, r):
        b_rims[i] = rows[r, 0]
        x_rims[i] = rows[r, 1]
        react_rims[i], upper_rims[i], lon_rims[i], lat_rims[i] = weigh(sets, rows[r, 2], 128)

    for r in range(RIM):
        take(r, rim_south, r)
        take(r + RIM + ROWS, rim_north, r)
    for r in range(ROWS):
        take(r + RIM, rim, r)

    def face_east(i):
        here = lon_weight[i]
        east[i] = 0.5 * (here + next_lane(here))
        upper[i] = upper_in[i]

    face_east(0)
    face_east(EXT - 1)

    def face(i):
        closed = (south_end & (i == RIM - 1)) | (north_end & (i == RIM + ROWS - 1))
        north[i] = jnp.where(closed, 0.0, 0.5) * (lat_weight[i] + lat_weight[i + 1])

    face(0)

    def start(i):
        face(i)
        face_east(i)
        at_end = (south_end & (i == RIM)) | (north_end & (i == RIM + ROWS - 1))
        whole = react_in[i] + jnp.where(at_end, 0.5, 0.0) * lat_weight[i]
        react[i] = whole
        whole = whole + east[i] + prev_lane(east[i]) + north[i] + north[i - 1]
        whole = whole + upper[i] + prev_level(upper[i])
        diag[i] = whole
        inverse = DAMP / whole
        winv[i] = inverse
        left = b[i] - (whole * x[i] - around(x, i, east, north, upper, 1))
        s[i] = left
        e0[i] = inverse * left

    loop(1, EXT - 1, start)

    north1[0] = 0.25 * pair_sum(north[1], even)

    def middle(m):
        i = 2 * m
        react1[m] = 0.25 * pair_sum(react[i] + react[i + 1], even)
        upper1[m] = 0.25 * pair_sum(upper[i] + upper[i + 1], even)
        eastern = east[i] + east[i + 1]
        east1[m] = 0.25 * jnp.where(even, next_lane(eastern), eastern)
        north1[m] = 0.25 * pair_sum(north[i + 1], even)
        whole = react1[m] + east1[m] + prev_lane(east1[m], 2) + north1[m] + north1[m - 1]
        inverse = DAMP / (whole + upper1[m] + prev_level(upper1[m]))
        winv1[m] = inverse
        restrict(m, s, e0, f1, e1, inverse, east, north, upper, even)

    loop(1, MID - 1, middle)

    last_of_four = lane % 4 == 3
    for c in range(2):
        m = 2 + 2 * c
        stage[c] = 0.125 * (react1[m] + react1[m + 1])
        stage[2 + c] = 0.125 * (upper1[m] + upper1[m + 1])
        stage[4 + c] = jnp.where(last_of_four, 0.25 * (east1[m] + east1[m + 1]), 0.0)
        left = middle_left(m, f1, e1, east1, north1, upper1)
        stage[6 + c] = 0.125 * (left + middle_left(m + 1, f1, e1, east1, north1, upper1))
    for c in range(3):
        stage[8 + c] = 0.125 * north1[1 + 2 * c]
    packed = times_blocks(stage[...].reshape(11 * LEV, LANES), blocks, 0).reshape(11, LEV, COLS)
    col = lax.broadcasted_iota(jnp.int32, (LEV, COLS), 1)
    empty = (col >= OWN_COLS + HALF_COLS) & (col < COLS - HALF_COLS)
    for c in range(2):
        upper2, east2, north2 = packed[2 + c], packed[4 + c], packed[9 + c]
        whole = packed[c] + east2 + prev_lane(east2) + north2 + packed[8 + c]
        whole = whole + upper2 + prev_level(upper2)
        weights2[0, 2 + c] = DAMP / jnp.where(empty, 1.0, whole)
        weights2[1, 2 + c] = east2
        weights2[2, 2 + c] = north2
        weights2[3, 2 + c] = upper2
    weights2[2, 1] = packed[8]
    f2 = (packed[6], packed[7])
    f2_out[0], f2_out[1] = f2
    hand_out(f2, (weights2[0, 2] * f2[0], weights2[0, 3] * f2[1]), weights2, to_north, to_south)


def sweep(k, f2, now, weights2):
    return KEEP * now[k] + weights2[0, k] * (
        f2[k] + around(now, k, weights2.at[1], weights2.at[2], weights2.at[3], 1)
    )


def two_sweeps(mine, north, south, weights2, f2, now, later):
    f2[1], f2[2], f2[3], f2[4] = south[0], mine[0], mine[1], north[0]
    now[0], now[5] = south[1], north[1]
    for k in range(1, 5):
        now[k] = weights2[0, k] * f2[k]
    for k in range(1, 5):
        later[k] = sweep(k, f2, now, weights2)
    return sweep(2, f2, later, weights2), sweep(3, f2, later, weights2)


def hand_on(e2, e1, to_north, to_south):
    for to, m in ((to_north, 4), (to_south, 3)):
        to[:, :COLS] = e2[0]
        to[:, COLS:2 * COLS] = e2[1]
        to[:, 2 * COLS:] = e1[m]


def coarse_kernel(mine, from_north, from_south, weights2, e1, f2, e2, to_north, to_south, whole2, now, later):
    for kind in range(4):
        for k in (2, 3):
            whole2[kind, k] = weights2[kind, k]
    for j, kind in enumerate((0, 1, 3)):
        whole2[kind, 1] = from_south[2 + j]
        whole2[kind, 4] = from_north[2 + j]
    whole2[2, 0], whole2[2, 1], whole2[2, 4] = from_south[5], weights2[2, 1], from_north[5]
    e2[0], e2[1] = two_sweeps(mine, from_north, from_south, whole2, f2, now, later)
    hand_on(e2, e1, to_north, to_south)


def coarse_dot_kernel(
    mine, from_north, from_south, weights2, e1, sums, sum_wq, f2, e2, to_north, to_south, dots, now, later
):
    e2[0], e2[1] = two_sweeps(mine, from_north, from_south, weights2, f2, now, later)
    hand_on(e2, e1, to_north, to_south)
    total = jnp.zeros((LEV, OWN_COLS), F32)
    for r in range(2):
        k = 2 + r
        first = now[k]
        once, twice = later[k], e2[r]
        term = f2[k] * once + (once - first) * (twice - first) / weights2[0, k]
        total = total + term[:, :OWN_COLS]
    column = lax.broadcasted_iota(jnp.int32, dots.shape, 1)
    line = jnp.where(column == 0, jnp.sum(sums[0]), 0.0) + jnp.where(column == 1, jnp.sum(sums[1]), 0.0)
    dots[...] = line + jnp.where(column == 2, jnp.sum(sum_wq[...]) + 16.0 * jnp.sum(total), 0.0)


def ascend(
    e2, from_north, from_south, f2, weights2, blocks, first, end, f, e0, f1, e1, winv, east, north, upper,
    winv1, east1, north1, upper1, now, sum1, sum0, result,
):
    for r in range(2):
        cols = slice(r * COLS, (r + 1) * COLS)
        now[r], now[2 + r], now[4 + r] = from_south[:, cols], e2[r], from_north[:, cols]
    rows = jnp.concatenate([sweep(k, f2, now, weights2) for k in range(1, 5)], axis=0)
    wide = times_blocks(rows, blocks, 1).reshape(4, LEV, LANES)
    for m in range(1, MID - 1):
        sum1[m] = e1[m] + wide[m // 2]
    sum1[0] = from_south[:, 2 * COLS:] + wide[0]
    sum1[MID - 1] = from_north[:, 2 * COLS:] + wide[3]

    def middle(m):
        better = KEEP * sum1[m] + winv1[m] * (f1[m] + around(sum1, m, east1, north1, upper1, 2))
        sum0[2 * m] = e0[2 * m] + better
        sum0[2 * m + 1] = e0[2 * m + 1] + better

    loop(1, MID - 1, middle)

    def fine(i):
        result[i] = KEEP * sum0[i] + winv[i] * (f[i] + around(sum0, i, east, north, upper, 1))

    loop(first, end, fine)


def first_up_kernel(
    e2, from_north, from_south, f2, weights2, blocks,
    s, e0, f1, e1, winv, east, north, upper, winv1, east1, north1, upper1, diag,
    p_own, w_own, w_north, w_south, s_own, sums,
    now, sum1, sum0, p,
):
    ascend(
        e2, from_north, from_south, f2, weights2, blocks, RIM - 1, RIM + ROWS + 1, s, e0, f1, e1, winv, east, north, upper,
        winv1, east1, north1, upper1, now, sum1, sum0, p,
    )

    def image(r, totals):
        i = r + RIM
        w_row = diag[i] * p[i] - around(p, i, east, north, upper, 1)
        w_own[r] = w_row
        p_row, s_row = p[i, :, :OWN], s[i, :, :OWN]
        p_own[r] = p_row
        s_own[r] = s_row
        return totals[0] + s_row * p_row, totals[1] + p_row * w_row[:, :OWN]

    zero = jnp.zeros((LEV, OWN), F32)
    sums[0], sums[1] = lax.fori_loop(0, ROWS, image, (zero, zero), unroll=4)
    w_south[...] = w_own[:SEND]
    w_north[...] = w_own[ROWS - SEND:]


def second_down_kernel(
    w_own, from_north, from_south, weights2, blocks, winv, east, north, upper, winv1, east1, north1, upper1,
    f2_out, to_north, to_south, e0, f1, e1, sum_wq,
    w, stage,
):
    even = lane_ids() % 2 == 0
    w[RIM - SEND:RIM] = from_south[...]
    w[RIM + ROWS:RIM + ROWS + SEND] = from_north[...]
    for r in range(ROWS):
        w[RIM + r] = w_own[r]

    def smooth(i):
        e0[i] = winv[i] * w[i]

    loop(1, EXT - 1, smooth)

    def down(m):
        return restrict(m, w, e0, f1, e1, winv1[m], east, north, upper, even)

    down(1)
    down(MID - 2)

    def down_own(m, total):
        left_0, left_1 = down(m)
        i = 2 * m
        term = e0[i] * (w[i] + left_0) + e0[i + 1] * (w[i + 1] + left_1)
        return total + term[:, :OWN]

    total = lax.fori_loop(2, 6, down_own, jnp.zeros((LEV, OWN), F32), unroll=4)
    for c in range(2):
        pair = 0.0
        for m in (2 + 2 * c, 3 + 2 * c):
            left = middle_left(m, f1, e1, east1, north1, upper1)
            total = total + 2.0 * (e1[m] * (f1[m] + left))[:, :OWN]
            pair = pair + left
        stage[c] = 0.125 * pair
    sum_wq[...] = total
    packed = times_blocks(stage[...].reshape(2 * LEV, LANES), blocks, 0).reshape(2, LEV, COLS)
    f2 = (packed[0], packed[1])
    f2_out[0], f2_out[1] = f2
    hand_out(f2, (weights2[0, 2] * f2[0], weights2[0, 3] * f2[1]), weights2, to_north, to_south)


def second_up_kernel(
    e2, from_north, from_south, f2, weights2, blocks,
    w_own, e0, f1, e1, winv, east, north, upper, winv1, east1, north1, upper1, dots,
    q_out, dots_out,
    now, sum1, sum0, w, result,
):
    for r in range(ROWS):
        w[RIM + r] = w_own[r]
    ascend(
        e2, from_north, from_south, f2, weights2, blocks, RIM, RIM + ROWS, w, e0, f1, e1, winv, east, north, upper,
        winv1, east1, north1, upper1, now, sum1, sum0, result,
    )
    dots_out[...] = dots[...]
    q_out[...] = jnp.swapaxes(result[RIM:RIM + ROWS, :, :OWN], 0, 1)


def turn_kernel(p, w, s, p_out, w_out, s_out):
    p_out[...] = jnp.swapaxes(p[...], 0, 1)
    w_out[...] = jnp.swapaxes(w[:, :, :OWN], 0, 1)
    s_out[...] = jnp.swapaxes(s[...], 0, 1)


def total_kernel(lines, total):
    total[...] = jnp.broadcast_to(jnp.sum(lines[...], axis=0, keepdims=True), total.shape)


def finish_kernel(dots, x, p, w, q, s, iterate, residual, direction):
    line = jnp.sum(dots[...], axis=0, keepdims=True)
    column = lax.broadcasted_iota(jnp.int32, (1, 128), 1)
    sp, pw, wq = [jnp.sum(jnp.where(column == j, line, 0.0), axis=1, keepdims=True)[None] for j in range(3)]
    step = sp / pw
    next_dot = (sp - step * pw) - step * (pw - step * wq)
    ratio = next_dot / sp
    iterate[...] = x[...] + step * p[...]
    residual[...] = s[...] - step * w[...]
    direction[...] = (p[...] - step * q[...]) + ratio * p[...]


def shards(right_side, initial_guess, land_mask, coefficient_sets):
    z_size, lat_size = lax.axis_size("z"), lax.axis_size("lat")
    lines = (lax.axis_size("x") * lat_size, 128)
    lon = ("x", "z")
    sizes = {lon: lax.axis_size("x") * z_size, "lat": lat_size}

    def trade(to_next, to_last, axis):
        size = sizes[axis]
        up = [(i, (i + 1) % size) for i in range(size)]
        from_last = lax.ppermute(to_next, axis, up)
        return lax.ppermute(to_last, axis, [(j, i) for i, j in up]), from_last

    row, fine, mid, line = (LEV, LANES), (EXT, LEV, LANES), (MID, LEV, LANES), (LEV, COLS)
    fields = [right_side, initial_guess, land_mask]
    blocks = blocks_matrix()
    to_north, to_south, to_east, to_west = call(
        pack_kernel,
        [(RIM, 3, LEV, OWN)] * 2 + [(ROWS, LEV, 128)] * 2,
        fields,
        [(3, LEV, ROWS, OWN), (3, ROWS, LEV, 256)],
        specs=[HBM] * 3,
        copies=3,
    )
    lat_rows = trade(to_north, to_south, "lat")
    lon_rims = trade(to_east, to_west, lon)
    rim, to_north, to_south = call(
        rim_kernel, [(ROWS, 3, LEV, 128), (RIM, 3, LEV, 128), (RIM, 3, LEV, 128)], lon_rims
    )
    lat_rims = trade(to_north, to_south, "lat")
    sea, land = coefficient_sets[0], coefficient_sets[1]
    sets = jnp.broadcast_to(jnp.concatenate([sea, land - sea])[:, :, None], (8, LEV, 128))

    main, side = (EXT, LEV, OWN), (EXT, LEV, 128)
    weighed = call(weigh_kernel, [main] * 6, fields + [*lat_rows, sets], [(ROWS, LEV, OWN)])
    (s, f2, to_north, to_south, weights2, e0, f1, e1, east, north, upper, winv, diag, east1, north1, upper1, winv1) = call(
        first_down_kernel,
        [fine, (2,) + line, (6,) + line, (6,) + line, (4, NEAR) + line, fine, mid, mid, fine, fine, fine, fine, fine, mid, mid, mid, mid],
        [*weighed, rim, *lat_rims, sets, blocks],
        [side] * 6 + [fine, mid, (11,) + row],
    )
    grids = [winv, east, north, upper, winv1, east1, north1, upper1]
    near = (NEAR,) + line
    edge = (LEV, 2 * COLS + LANES)
    f2_near, e2, edge_north, edge_south, weights2 = call(
        coarse_kernel,
        [near, (2,) + line, edge, edge, (4, NEAR) + line],
        [f2, *trade(to_north, to_south, "lat"), weights2, e1],
        [near, near],
    )
    p_own, w_own, to_north, to_south, s_own, sums = call(
        first_up_kernel,
        [(ROWS, LEV, OWN), (ROWS,) + row, (SEND,) + row, (SEND,) + row, (ROWS, LEV, OWN), (2, LEV, OWN)],
        [e2, *trade(edge_north, edge_south, "lat"), f2_near, weights2, blocks, s, e0, f1, e1] + grids + [diag],
        [near, mid, fine, fine],
    )
    w_rows = trade(to_north, to_south, "lat")
    p, w, s = call(turn_kernel, [(LEV, ROWS, OWN)] * 3, [p_own, w_own, s_own])
    f2, to_north, to_south, e0, f1, e1, sum_wq = call(
        second_down_kernel,
        [(2,) + line] * 3 + [fine, mid, mid, (LEV, OWN)],
        [w_own, *w_rows, weights2, blocks] + grids,
        [fine, (2,) + row],
    )
    f2_near, e2, edge_north, edge_south, dots = call(
        coarse_dot_kernel,
        [near, (2,) + line, edge, edge, lines],
        [f2, *trade(to_north, to_south, "lat"), weights2, e1, sums, sum_wq],
        [near, near],
    )
    q, dots = call(
        second_up_kernel,
        [(LEV, ROWS, OWN), lines],
        [e2, *trade(edge_north, edge_south, "lat"), f2_near, weights2, blocks, w_own, e0, f1, e1] + grids + [dots],
        [near, mid, fine, fine, fine],
    )
    (dots,) = call(total_kernel, [(z_size, 128)], [lax.all_to_all(dots, ("x", "lat"), 0, 0, tiled=True)])
    dots = lax.all_to_all(dots, "z", 0, 0, tiled=True)
    return tuple(call(finish_kernel, [(LEV, ROWS, OWN)] * 3, [dots, initial_guess, p, w, q, s]))


def solution(mesh):
    lon, lat = mesh.shape["lon"], mesh.shape["lat"]
    z = 16 if lon % 16 == 0 else lon
    grid = jax.sharding.Mesh(mesh.devices.reshape(lon // z, z, lat), ("x", "z", "lat"))
    field = P(None, "lat", ("x", "z"))
    return jax.shard_map(
        shards, mesh=grid, in_specs=(field, field, field, P()), out_specs=(field, field, field), check_vma=False
    )
```

```python
import jax
import jax.numpy as jnp
import numpy as np
from jax import lax
from jax.experimental import pallas as pl
from jax.experimental.pallas import tpu as pltpu
from jax.sharding import PartitionSpec as P


LEV = 16
ROWS = 8
OWN = 512
HALF = 64
DEEP = 42
LANES = OWN + 2 * HALF
RIM = 4
EXT = ROWS + 2 * RIM
MID = EXT // 2
SEND = 3
NEAR = 6
COLS = 256
OWN_COLS = OWN // 4
HALF_COLS = HALF // 4
DAMP = 0.8
KEEP = 1.0 - DAMP
F32 = jnp.float32

VMEM = pl.BlockSpec(memory_space=pltpu.VMEM)
HBM = pl.BlockSpec(memory_space=pltpu.HBM)


def call(body, outs, ins, scratch=(), specs=(), copies=0, out_spec=VMEM):
    return pl.pallas_call(
        body,
        out_shape=[jax.ShapeDtypeStruct(o, F32) for o in outs],
        in_specs=list(specs) + [VMEM] * (len(ins) - len(specs)),
        out_specs=[out_spec] * len(outs),
        scratch_shapes=[pltpu.VMEM(s, F32) for s in scratch] + [pltpu.SemaphoreType.DMA((copies,))] * (copies > 0),
        compiler_params=pltpu.CompilerParams(vmem_limit_bytes=(60 if copies else 24) * 1024 * 1024),
        cost_estimate=pl.CostEstimate(flops=1000000, bytes_accessed=1000000, transcendentals=0),
    )(*ins)


def loop(first, end, body):
    def step(i, carry):
        body(i)
        return carry

    lax.fori_loop(first, end, step, 0, unroll=True)


def lane_ids():
    return lax.broadcasted_iota(jnp.int32, (LEV, LANES), 1)


def next_lane(v, n=1):
    return pltpu.roll(v, v.shape[-1] - n, axis=1)


def prev_lane(v, n=1):
    return pltpu.roll(v, n, axis=1)


def next_level(v):
    return pltpu.roll(v, LEV - 1, axis=0)


def prev_level(v):
    return pltpu.roll(v, 1, axis=0)


def pair_sum(v, even):
    return v + jnp.where(even, next_lane(v), prev_lane(v))


def around(v, i, east, north, upper, n):
    here = v[i]
    total = east[i] * next_lane(here, n) + prev_lane(east[i] * here, n)
    total = total + upper[i] * next_level(here) + prev_level(upper[i] * here)
    return total + north[i] * v[i + 1] + north[i - 1] * v[i - 1]


def blocks_matrix():
    lane = np.arange(LANES)
    cell = lane // 4
    cell = np.where(cell < OWN_COLS + HALF_COLS, cell, cell + COLS - LANES // 4)
    matrix = np.zeros((LANES, COLS), np.float32)
    matrix[lane, cell] = 1.0
    return jnp.asarray(matrix, jnp.bfloat16)


def times_blocks(rows, blocks, side):
    total = 0.0
    left = rows
    for _ in range(3):
        part = left.astype(jnp.bfloat16)
        left = left - part.astype(F32)
        total = total + lax.dot_general(part, blocks[...], (((1,), (side,)), ((), ())), preferred_element_type=F32)
    return total


def pack_kernel(
    b_ref, x_ref, c_ref, to_north, to_south, to_east, to_west,
    held, turned, north_ref, south_ref, east_ref, west_ref, moved,
):
    lane = lax.broadcasted_iota(jnp.int32, (LEV, 128), 1)
    copies = [pltpu.make_async_copy(ref, held.at[j], moved.at[j]) for j, ref in enumerate((b_ref, x_ref, c_ref))]
    for copy in copies:
        copy.start()
    for j, copy in enumerate(copies):
        copy.wait()
        field = jnp.swapaxes(held[j], 0, 1)
        turned[j, :, :, :128] = field[:, :, :128]
        turned[j, :, :, 128:] = field[:, :, OWN - 128:]
        south_ref[:, j] = field[:RIM]
        north_ref[:, j] = field[ROWS - RIM:]
    results = ((north_ref, to_north), (south_ref, to_south), (east_ref, to_east), (west_ref, to_west))
    copies = [pltpu.make_async_copy(a, b, moved.at[3 + j]) for j, (a, b) in enumerate(results)]
    copies[0].start()
    copies[1].start()
    for r in range(ROWS):
        b, x, c = [turned[j, r, :, :128] for j in range(3)]
        west_ref[r] = jnp.where(lane < DEEP, b, jnp.where(lane < 2 * DEEP, prev_lane(x, DEEP), prev_lane(c, 2 * DEEP)))
        b, x, c = [turned[j, r, :, 128:] for j in range(3)]
        x, c = next_lane(x, DEEP), next_lane(c, 2 * DEEP)
        east_ref[r] = jnp.where(lane >= 128 - DEEP, b, jnp.where(lane >= 128 - 2 * DEEP, x, c))
    copies[2].start()
    copies[3].start()
    for copy in copies:
        copy.wait()


def rim_kernel(from_east, from_west, rim_ref, north_ref, south_ref):
    lane = lax.broadcasted_iota(jnp.int32, (LEV, 128), 1)
    for r in range(ROWS):
        east, west = from_east[r], from_west[r]
        for j in range(3):
            if j > 0:
                east, west = next_lane(east, DEEP), prev_lane(west, DEEP)
            rim_ref[r, j] = jnp.where(lane < DEEP, east, jnp.where(lane >= 128 - DEEP, west, 0.0))
    south_ref[...] = rim_ref[:RIM]
    north_ref[...] = rim_ref[ROWS - RIM:]


def restrict(m, f, e0, f1, e1, winv1, east, north, upper, even):
    i = 2 * m
    left_0 = KEEP * f[i] + around(e0, i, east, north, upper, 1)
    left_1 = KEEP * f[i + 1] + around(e0, i + 1, east, north, upper, 1)
    rhs = 0.25 * pair_sum(left_0 + left_1, even)
    f1[m] = rhs
    e1[m] = winv1 * rhs
    return left_0, left_1


def middle_left(m, f1, e1, east1, north1, upper1):
    return KEEP * f1[m] + around(e1, m, east1, north1, upper1, 2)


def hand_out(f2, e2, weights2, to_north, to_south):
    to_north[0], to_north[1] = f2[1], e2[0]
    to_south[0], to_south[1] = f2[0], e2[1]
    if to_north.shape[0] > 2:
        for j, kind in enumerate((0, 1, 3)):
            to_north[2 + j] = weights2[kind, 3]
            to_south[2 + j] = weights2[kind, 2]
        to_north[5] = weights2[2, 2]
        to_south[5] = weights2[2, 2]


def weigh(sets, share, width):
    level = lax.broadcasted_iota(jnp.int32, (LEV, width), 0)
    top = level == LEV - 1
    edge = top | (level == 0)

    def blend(column):
        sea = jnp.concatenate([sets[column]] * (width // 128), axis=1)
        return sea + share * jnp.concatenate([sets[column + 4]] * (width // 128), axis=1)

    lev_weight = blend(3)
    react = blend(0) + jnp.where(edge, 0.5 * lev_weight, 0.0)
    upper = jnp.where(top, 0.0, 0.5 * (lev_weight + next_level(lev_weight)))
    return react, upper, blend(1), blend(2)


def weigh_kernel(
    b_ref, x_ref, c_ref, from_north, from_south, sets,
    b, x, react, upper, lon_weight, lat_weight,
    share,
):
    share[...] = jnp.swapaxes(c_ref[...], 0, 1)
    b[RIM:RIM + ROWS] = jnp.swapaxes(b_ref[...], 0, 1)
    x[RIM:RIM + ROWS] = jnp.swapaxes(x_ref[...], 0, 1)

    def own(r):
        i = r + RIM
        react[i], upper[i], lon_weight[i], lat_weight[i] = weigh(sets, share[r], OWN)

    def outer(i, rows, r):
        b[i] = rows[r, 0]
        x[i] = rows[r, 1]
        react[i], upper[i], lon_weight[i], lat_weight[i] = weigh(sets, rows[r, 2], OWN)

    loop(0, ROWS, own)
    loop(0, RIM, lambda r: outer(r, from_south, r))
    loop(0, RIM, lambda r: outer(r + RIM + ROWS, from_north, r))


class Joined:
    def __init__(self, main, rims):
        self.main, self.rims = main, rims

    def __getitem__(self, i):
        return jnp.concatenate([self.main[i], self.rims[i]], axis=1)


def first_down_kernel(
    b_main, x_main, react_main, upper_main, lon_main, lat_main, rim, rim_north, rim_south, sets, blocks,
    s, f2_out, to_north, to_south, weights2, e0, f1, e1, east, north, upper, winv, diag, east1, north1, upper1, winv1,
    b_rims, x_rims, react_rims, upper_rims, lon_rims, lat_rims, react, react1, stage,
):
    b, x, react_in = Joined(b_main, b_rims), Joined(x_main, x_rims), Joined(react_main, react_rims)
    upper_in, lon_weight, lat_weight = Joined(upper_main, upper_rims), Joined(lon_main, lon_rims), Joined(lat_main, lat_rims)
    lane = lane_ids()
    even = lane % 2 == 0
    lat = lax.axis_index("lat")
    south_end = lat == 0
    north_end = lat == lax.axis_size("lat") - 1

    def take(i, rows, r):
        b_rims[i] = rows[r, 0]
        x_rims[i] = rows[r, 1]
        react_rims[i], upper_rims[i], lon_rims[i], lat_rims[i] = weigh(sets, rows[r, 2], 128)

    for r in range(RIM):
        take(r, rim_south, r)
        take(r + RIM + ROWS, rim_north, r)
    for r in range(ROWS):
        take(r + RIM, rim, r)

    def face_east(i):
        here = lon_weight[i]
        east[i] = 0.5 * (here + next_lane(here))
        upper[i] = upper_in[i]

    face_east(0)
    face_east(EXT - 1)

    def face(i):
        closed = (south_end & (i == RIM - 1)) | (north_end & (i == RIM + ROWS - 1))
        north[i] = jnp.where(closed, 0.0, 0.5) * (lat_weight[i] + lat_weight[i + 1])

    face(0)

    def start(i):
        face(i)
        face_east(i)
        at_end = (south_end & (i == RIM)) | (north_end & (i == RIM + ROWS - 1))
        whole = react_in[i] + jnp.where(at_end, 0.5, 0.0) * lat_weight[i]
        react[i] = whole
        whole = whole + east[i] + prev_lane(east[i]) + north[i] + north[i - 1]
        whole = whole + upper[i] + prev_level(upper[i])
        diag[i] = whole
        inverse = DAMP / whole
        winv[i] = inverse
        left = b[i] - (whole * x[i] - around(x, i, east, north, upper, 1))
        s[i] = left
        e0[i] = inverse * left

    loop(1, EXT - 1, start)

    north1[0] = 0.25 * pair_sum(north[1], even)

    def middle(m):
        i = 2 * m
        react1[m] = 0.25 * pair_sum(react[i] + react[i + 1], even)
        upper1[m] = 0.25 * pair_sum(upper[i] + upper[i + 1], even)
        eastern = east[i] + east[i + 1]
        east1[m] = 0.25 * jnp.where(even, next_lane(eastern), eastern)
        north1[m] = 0.25 * pair_sum(north[i + 1], even)
        whole = react1[m] + east1[m] + prev_lane(east1[m], 2) + north1[m] + north1[m - 1]
        inverse = DAMP / (whole + upper1[m] + prev_level(upper1[m]))
        winv1[m] = inverse
        restrict(m, s, e0, f1, e1, inverse, east, north, upper, even)

    loop(1, MID - 1, middle)

    last_of_four = lane % 4 == 3
    for c in range(2):
        m = 2 + 2 * c
        stage[c] = 0.125 * (react1[m] + react1[m + 1])
        stage[2 + c] = 0.125 * (upper1[m] + upper1[m + 1])
        stage[4 + c] = jnp.where(last_of_four, 0.25 * (east1[m] + east1[m + 1]), 0.0)
        left = middle_left(m, f1, e1, east1, north1, upper1)
        stage[6 + c] = 0.125 * (left + middle_left(m + 1, f1, e1, east1, north1, upper1))
    for c in range(3):
        stage[8 + c] = 0.125 * north1[1 + 2 * c]
    packed = times_blocks(stage[...].reshape(11 * LEV, LANES), blocks, 0).reshape(11, LEV, COLS)
    col = lax.broadcasted_iota(jnp.int32, (LEV, COLS), 1)
    empty = (col >= OWN_COLS + HALF_COLS) & (col < COLS - HALF_COLS)
    for c in range(2):
        upper2, east2, north2 = packed[2 + c], packed[4 + c], packed[9 + c]
        whole = packed[c] + east2 + prev_lane(east2) + north2 + packed[8 + c]
        whole = whole + upper2 + prev_level(upper2)
        weights2[0, 2 + c] = DAMP / jnp.where(empty, 1.0, whole)
        weights2[1, 2 + c] = east2
        weights2[2, 2 + c] = north2
        weights2[3, 2 + c] = upper2
    weights2[2, 1] = packed[8]
    f2 = (packed[6], packed[7])
    f2_out[0], f2_out[1] = f2
    hand_out(f2, (weights2[0, 2] * f2[0], weights2[0, 3] * f2[1]), weights2, to_north, to_south)


def sweep(k, f2, now, weights2):
    return KEEP * now[k] + weights2[0, k] * (
        f2[k] + around(now, k, weights2.at[1], weights2.at[2], weights2.at[3], 1)
    )


def two_sweeps(mine, north, south, weights2, f2, now, later):
    f2[1], f2[2], f2[3], f2[4] = south[0], mine[0], mine[1], north[0]
    now[0], now[5] = south[1], north[1]
    for k in range(1, 5):
        now[k] = weights2[0, k] * f2[k]
    for k in range(1, 5):
        later[k] = sweep(k, f2, now, weights2)
    return sweep(2, f2, later, weights2), sweep(3, f2, later, weights2)


def hand_on(e2, e1, to_north, to_south):
    for to, m in ((to_north, 4), (to_south, 3)):
        to[:, :COLS] = e2[0]
        to[:, COLS:2 * COLS] = e2[1]
        to[:, 2 * COLS:] = e1[m]


def coarse_kernel(mine, from_north, from_south, weights2, e1, f2, e2, to_north, to_south, whole2, now, later):
    for kind in range(4):
        for k in (2, 3):
            whole2[kind, k] = weights2[kind, k]
    for j, kind in enumerate((0, 1, 3)):
        whole2[kind, 1] = from_south[2 + j]
        whole2[kind, 4] = from_north[2 + j]
    whole2[2, 0], whole2[2, 1], whole2[2, 4] = from_south[5], weights2[2, 1], from_north[5]
    e2[0], e2[1] = two_sweeps(mine, from_north, from_south, whole2, f2, now, later)
    hand_on(e2, e1, to_north, to_south)


def coarse_dot_kernel(
    mine, from_north, from_south, weights2, e1, sums, sum_wq, f2, e2, to_north, to_south, dots, now, later
):
    e2[0], e2[1] = two_sweeps(mine, from_north, from_south, weights2, f2, now, later)
    hand_on(e2, e1, to_north, to_south)
    total = jnp.zeros((LEV, OWN_COLS), F32)
    for r in range(2):
        k = 2 + r
        first = now[k]
        once, twice = later[k], e2[r]
        term = f2[k] * once + (once - first) * (twice - first) / weights2[0, k]
        total = total + term[:, :OWN_COLS]
    column = lax.broadcasted_iota(jnp.int32, dots.shape, 1)
    line = jnp.where(column == 0, jnp.sum(sums[0]), 0.0) + jnp.where(column == 1, jnp.sum(sums[1]), 0.0)
    dots[...] = line + jnp.where(column == 2, jnp.sum(sum_wq[...]) + 16.0 * jnp.sum(total), 0.0)


def ascend(
    e2, from_north, from_south, f2, weights2, blocks, first, end, f, e0, f1, e1, winv, east, north, upper,
    winv1, east1, north1, upper1, now, sum1, sum0, result,
):
    for r in range(2):
        cols = slice(r * COLS, (r + 1) * COLS)
        now[r], now[2 + r], now[4 + r] = from_south[:, cols], e2[r], from_north[:, cols]
    rows = jnp.concatenate([sweep(k, f2, now, weights2) for k in range(1, 5)], axis=0)
    wide = times_blocks(rows, blocks, 1).reshape(4, LEV, LANES)
    for m in range(1, MID - 1):
        sum1[m] = e1[m] + wide[m // 2]
    sum1[0] = from_south[:, 2 * COLS:] + wide[0]
    sum1[MID - 1] = from_north[:, 2 * COLS:] + wide[3]

    def middle(m):
        better = KEEP * sum1[m] + winv1[m] * (f1[m] + around(sum1, m, east1, north1, upper1, 2))
        sum0[2 * m] = e0[2 * m] + better
        sum0[2 * m + 1] = e0[2 * m + 1] + better

    loop(1, MID - 1, middle)

    def fine(i):
        result[i] = KEEP * sum0[i] + winv[i] * (f[i] + around(sum0, i, east, north, upper, 1))

    loop(first, end, fine)


def first_up_kernel(
    e2, from_north, from_south, f2, weights2, blocks,
    s, e0, f1, e1, winv, east, north, upper, winv1, east1, north1, upper1, diag,
    p_own, w_own, w_north, w_south, s_own, sums,
    now, sum1, sum0, p,
):
    ascend(
        e2, from_north, from_south, f2, weights2, blocks, RIM - 1, RIM + ROWS + 1, s, e0, f1, e1, winv, east, north, upper,
        winv1, east1, north1, upper1, now, sum1, sum0, p,
    )

    def image(r, totals):
        i = r + RIM
        w_row = diag[i] * p[i] - around(p, i, east, north, upper, 1)
        w_own[r] = w_row
        p_row, s_row = p[i, :, :OWN], s[i, :, :OWN]
        p_own[r] = p_row
        s_own[r] = s_row
        return totals[0] + s_row * p_row, totals[1] + p_row * w_row[:, :OWN]

    zero = jnp.zeros((LEV, OWN), F32)
    sums[0], sums[1] = lax.fori_loop(0, ROWS, image, (zero, zero), unroll=True)
    w_south[...] = w_own[:SEND]
    w_north[...] = w_own[ROWS - SEND:]


def second_down_kernel(
    w_own, from_north, from_south, weights2, blocks, winv, east, north, upper, winv1, east1, north1, upper1,
    f2_out, to_north, to_south, e0, f1, e1, sum_wq,
    w, stage,
):
    even = lane_ids() % 2 == 0
    w[RIM - SEND:RIM] = from_south[...]
    w[RIM + ROWS:RIM + ROWS + SEND] = from_north[...]
    for r in range(ROWS):
        w[RIM + r] = w_own[r]

    def smooth(i):
        e0[i] = winv[i] * w[i]

    loop(1, EXT - 1, smooth)

    def down(m):
        return restrict(m, w, e0, f1, e1, winv1[m], east, north, upper, even)

    down(1)
    down(MID - 2)

    def down_own(m, total):
        left_0, left_1 = down(m)
        i = 2 * m
        term = e0[i] * (w[i] + left_0) + e0[i + 1] * (w[i + 1] + left_1)
        return total + term[:, :OWN]

    total = lax.fori_loop(2, 6, down_own, jnp.zeros((LEV, OWN), F32), unroll=4)
    for c in range(2):
        pair = 0.0
        for m in (2 + 2 * c, 3 + 2 * c):
            left = middle_left(m, f1, e1, east1, north1, upper1)
            total = total + 2.0 * (e1[m] * (f1[m] + left))[:, :OWN]
            pair = pair + left
        stage[c] = 0.125 * pair
    sum_wq[...] = total
    packed = times_blocks(stage[...].reshape(2 * LEV, LANES), blocks, 0).reshape(2, LEV, COLS)
    f2 = (packed[0], packed[1])
    f2_out[0], f2_out[1] = f2
    hand_out(f2, (weights2[0, 2] * f2[0], weights2[0, 3] * f2[1]), weights2, to_north, to_south)


def second_up_kernel(
    e2, from_north, from_south, f2, weights2, blocks,
    w_own, e0, f1, e1, winv, east, north, upper, winv1, east1, north1, upper1, dots,
    q_out, dots_out,
    now, sum1, sum0, w, result,
):
    for r in range(ROWS):
        w[RIM + r] = w_own[r]
    ascend(
        e2, from_north, from_south, f2, weights2, blocks, RIM, RIM + ROWS, w, e0, f1, e1, winv, east, north, upper,
        winv1, east1, north1, upper1, now, sum1, sum0, result,
    )
    dots_out[...] = dots[...]
    q_out[...] = jnp.swapaxes(result[RIM:RIM + ROWS, :, :OWN], 0, 1)


def turn_kernel(p, w, s, p_out, w_out, s_out):
    p_out[...] = jnp.swapaxes(p[...], 0, 1)
    w_out[...] = jnp.swapaxes(w[:, :, :OWN], 0, 1)
    s_out[...] = jnp.swapaxes(s[...], 0, 1)


def total_kernel(lines, total):
    total[...] = jnp.broadcast_to(jnp.sum(lines[...], axis=0, keepdims=True), total.shape)


def finish_kernel(dots, x, p, w, q, s, iterate, residual, direction):
    line = jnp.sum(dots[...], axis=0, keepdims=True)
    column = lax.broadcasted_iota(jnp.int32, (1, 128), 1)
    sp, pw, wq = [jnp.sum(jnp.where(column == j, line, 0.0), axis=1, keepdims=True)[None] for j in range(3)]
    step = sp / pw
    next_dot = (sp - step * pw) - step * (pw - step * wq)
    ratio = next_dot / sp
    iterate[...] = x[...] + step * p[...]
    residual[...] = s[...] - step * w[...]
    direction[...] = (p[...] - step * q[...]) + ratio * p[...]


def shards(right_side, initial_guess, land_mask, coefficient_sets):
    z_size, lat_size = lax.axis_size("z"), lax.axis_size("lat")
    lines = (lax.axis_size("x") * lat_size, 128)
    lon = ("x", "z")
    sizes = {lon: lax.axis_size("x") * z_size, "lat": lat_size}

    def trade(to_next, to_last, axis):
        size = sizes[axis]
        up = [(i, (i + 1) % size) for i in range(size)]
        from_last = lax.ppermute(to_next, axis, up)
        return lax.ppermute(to_last, axis, [(j, i) for i, j in up]), from_last

    row, fine, mid, line = (LEV, LANES), (EXT, LEV, LANES), (MID, LEV, LANES), (LEV, COLS)
    fields = [right_side, initial_guess, land_mask]
    blocks = blocks_matrix()
    to_north, to_south, to_east, to_west = call(
        pack_kernel,
        [(RIM, 3, LEV, OWN)] * 2 + [(ROWS, LEV, 128)] * 2,
        fields,
        [(3, LEV, ROWS, OWN), (3, ROWS, LEV, 256)] + [(RIM, 3, LEV, OWN)] * 2 + [(ROWS, LEV, 128)] * 2,
        specs=[HBM] * 3,
        copies=7,
        out_spec=HBM,
    )
    lat_rows = trade(to_north, to_south, "lat")
    lon_rims = trade(to_east, to_west, lon)
    rim, to_north, to_south = call(
        rim_kernel, [(ROWS, 3, LEV, 128), (RIM, 3, LEV, 128), (RIM, 3, LEV, 128)], lon_rims
    )
    lat_rims = trade(to_north, to_south, "lat")
    sea, land = coefficient_sets[0], coefficient_sets[1]
    sets = jnp.broadcast_to(jnp.concatenate([sea, land - sea])[:, :, None], (8, LEV, 128))

    main, side = (EXT, LEV, OWN), (EXT, LEV, 128)
    weighed = call(weigh_kernel, [main] * 6, fields + [*lat_rows, sets], [(ROWS, LEV, OWN)])
    (s, f2, to_north, to_south, weights2, e0, f1, e1, east, north, upper, winv, diag, east1, north1, upper1, winv1) = call(
        first_down_kernel,
        [fine, (2,) + line, (6,) + line, (6,) + line, (4, NEAR) + line, fine, mid, mid, fine, fine, fine, fine, fine, mid, mid, mid, mid],
        [*weighed, rim, *lat_rims, sets, blocks],
        [side] * 6 + [fine, mid, (11,) + row],
    )
    grids = [winv, east, north, upper, winv1, east1, north1, upper1]
    near = (NEAR,) + line
    edge = (LEV, 2 * COLS + LANES)
    f2_near, e2, edge_north, edge_south, weights2 = call(
        coarse_kernel,
        [near, (2,) + line, edge, edge, (4, NEAR) + line],
        [f2, *trade(to_north, to_south, "lat"), weights2, e1],
        [near, near],
    )
    p_own, w_own, to_north, to_south, s_own, sums = call(
        first_up_kernel,
        [(ROWS, LEV, OWN), (ROWS,) + row, (SEND,) + row, (SEND,) + row, (ROWS, LEV, OWN), (2, LEV, OWN)],
        [e2, *trade(edge_north, edge_south, "lat"), f2_near, weights2, blocks, s, e0, f1, e1] + grids + [diag],
        [near, mid, fine, fine],
    )
    w_rows = trade(to_north, to_south, "lat")
    p, w, s = call(turn_kernel, [(LEV, ROWS, OWN)] * 3, [p_own, w_own, s_own])
    f2, to_north, to_south, e0, f1, e1, sum_wq = call(
        second_down_kernel,
        [(2,) + line] * 3 + [fine, mid, mid, (LEV, OWN)],
        [w_own, *w_rows, weights2, blocks] + grids,
        [fine, (2,) + row],
    )
    f2_near, e2, edge_north, edge_south, dots = call(
        coarse_dot_kernel,
        [near, (2,) + line, edge, edge, lines],
        [f2, *trade(to_north, to_south, "lat"), weights2, e1, sums, sum_wq],
        [near, near],
    )
    q, dots = call(
        second_up_kernel,
        [(LEV, ROWS, OWN), lines],
        [e2, *trade(edge_north, edge_south, "lat"), f2_near, weights2, blocks, w_own, e0, f1, e1] + grids + [dots],
        [near, mid, fine, fine, fine],
    )
    (dots,) = call(total_kernel, [(z_size, 128)], [lax.all_to_all(dots, ("x", "lat"), 0, 0, tiled=True)])
    dots = lax.all_to_all(dots, "z", 0, 0, tiled=True)
    return tuple(call(finish_kernel, [(LEV, ROWS, OWN)] * 3, [dots, initial_guess, p, w, q, s]))


def solution(mesh):
    lon, lat = mesh.shape["lon"], mesh.shape["lat"]
    z = 16 if lon % 16 == 0 else lon
    grid = jax.sharding.Mesh(mesh.devices.reshape(lon // z, z, lat), ("x", "z", "lat"))
    field = P(None, "lat", ("x", "z"))
    return jax.shard_map(
        shards, mesh=grid, in_specs=(field, field, field, P()), out_specs=(field, field, field), check_vma=False
    )
```

```python
import jax
import jax.numpy as jnp
import numpy as np
from jax import lax
from jax.experimental import pallas as pl
from jax.experimental.pallas import tpu as pltpu
from jax.sharding import PartitionSpec as P


LEV = 16
ROWS = 8
OWN = 512
HALF = 64
DEEP = 42
LANES = OWN + 2 * HALF
RIM = 4
EXT = ROWS + 2 * RIM
MID = EXT // 2
SEND = 3
PLANES = 2 * RIM + SEND
NEAR = 6
COLS = 256
OWN_COLS = OWN // 4
HALF_COLS = HALF // 4
DAMP = 0.8
KEEP = 1.0 - DAMP
F32 = jnp.float32

VMEM = pl.BlockSpec(memory_space=pltpu.VMEM)
HBM = pl.BlockSpec(memory_space=pltpu.HBM)


def call(body, outs, ins, scratch=(), specs=(), copies=0, out_spec=VMEM):
    return pl.pallas_call(
        body,
        out_shape=[jax.ShapeDtypeStruct(o, F32) for o in outs],
        in_specs=list(specs) + [VMEM] * (len(ins) - len(specs)),
        out_specs=[out_spec] * len(outs),
        scratch_shapes=[pltpu.VMEM(s, F32) for s in scratch] + [pltpu.SemaphoreType.DMA((copies,))] * (copies > 0),
        compiler_params=pltpu.CompilerParams(vmem_limit_bytes=(60 if copies else 24) * 1024 * 1024),
        cost_estimate=pl.CostEstimate(flops=1000000, bytes_accessed=1000000, transcendentals=0),
    )(*ins)


def loop(first, end, body):
    for i in range(first, end):
        body(i)


def lane_ids():
    return lax.broadcasted_iota(jnp.int32, (LEV, LANES), 1)


def next_lane(v, n=1):
    return pltpu.roll(v, v.shape[-1] - n, axis=1)


def prev_lane(v, n=1):
    return pltpu.roll(v, n, axis=1)


def next_level(v):
    return pltpu.roll(v, LEV - 1, axis=0)


def prev_level(v):
    return pltpu.roll(v, 1, axis=0)


def pair_sum(v, even):
    return v + jnp.where(even, next_lane(v), prev_lane(v))


def around(v, i, east, north, upper, n):
    here = v[i]
    total = east[i] * next_lane(here, n) + prev_lane(east[i] * here, n)
    total = total + upper[i] * next_level(here) + prev_level(upper[i] * here)
    return total + north[i] * v[i + 1] + north[i - 1] * v[i - 1]


def blocks_matrix():
    lane = np.arange(LANES)
    cell = lane // 4
    cell = np.where(cell < OWN_COLS + HALF_COLS, cell, cell + COLS - LANES // 4)
    matrix = np.zeros((LANES, COLS), np.float32)
    matrix[lane, cell] = 1.0
    return jnp.asarray(matrix, jnp.bfloat16)


def times_blocks(rows, blocks, side):
    total = 0.0
    left = rows
    for _ in range(3):
        part = left.astype(jnp.bfloat16)
        left = left - part.astype(F32)
        total = total + lax.dot_general(part, blocks[...], (((1,), (side,)), ((), ())), preferred_element_type=F32)
    return total


def put_planes(j, rows, north_ref, south_ref):
    count = RIM if j else SEND
    first = (j - 1) * RIM if j else 2 * RIM
    south_ref[first:first + count] = rows(0, count)
    north_ref[first:first + count] = rows(ROWS - count, ROWS)


def outer_planes(from_north, from_south):
    for r in range(RIM):
        b = from_south[2 * RIM + r - 1] if r >= RIM - SEND else None
        yield r, b, from_south[r], from_south[RIM + r]
        b = from_north[2 * RIM + r] if r < SEND else None
        yield RIM + ROWS + r, b, from_north[r], from_north[RIM + r]


def pack_kernel(
    b_ref, x_ref, c_ref, to_north, to_south, to_east, to_west,
    held, turned, north_ref, south_ref, east_ref, west_ref, moved,
):
    lane = lax.broadcasted_iota(jnp.int32, (LEV, 128), 1)
    copies = [pltpu.make_async_copy(ref, held.at[j], moved.at[j]) for j, ref in enumerate((b_ref, x_ref, c_ref))]
    for copy in copies:
        copy.start()
    for j, copy in enumerate(copies):
        copy.wait()
        field = jnp.swapaxes(held[j], 0, 1)
        turned[j, :, :, :128] = field[:, :, :128]
        turned[j, :, :, 128:] = field[:, :, OWN - 128:]
        put_planes(j, lambda first, end: field[first:end], north_ref, south_ref)
    results = ((north_ref, to_north), (south_ref, to_south), (east_ref, to_east), (west_ref, to_west))
    copies = [pltpu.make_async_copy(a, b, moved.at[3 + j]) for j, (a, b) in enumerate(results)]
    copies[0].start()
    copies[1].start()
    for r in range(ROWS):
        b, x, c = [turned[j, r, :, :128] for j in range(3)]
        west_ref[r] = jnp.where(lane < DEEP, b, jnp.where(lane < 2 * DEEP, prev_lane(x, DEEP), prev_lane(c, 2 * DEEP)))
        b, x, c = [turned[j, r, :, 128:] for j in range(3)]
        x, c = next_lane(x, DEEP), next_lane(c, 2 * DEEP)
        east_ref[r] = jnp.where(lane >= 128 - DEEP, b, jnp.where(lane >= 128 - 2 * DEEP, x, c))
    copies[2].start()
    copies[3].start()
    for copy in copies:
        copy.wait()


def rim_kernel(from_east, from_west, rim_ref, north_ref, south_ref):
    lane = lax.broadcasted_iota(jnp.int32, (LEV, 128), 1)
    for r in range(ROWS):
        east, west = from_east[r], from_west[r]
        for j in range(3):
            if j > 0:
                east, west = next_lane(east, DEEP), prev_lane(west, DEEP)
            rim_ref[r, j] = jnp.where(lane < DEEP, east, jnp.where(lane >= 128 - DEEP, west, 0.0))
    for j in range(3):
        put_planes(j, lambda first, end: rim_ref[first:end, j], north_ref, south_ref)


def restrict(m, f, e0, f1, e1, winv1, east, north, upper, even):
    i = 2 * m
    left_0 = KEEP * f[i] + around(e0, i, east, north, upper, 1)
    left_1 = KEEP * f[i + 1] + around(e0, i + 1, east, north, upper, 1)
    rhs = 0.25 * pair_sum(left_0 + left_1, even)
    f1[m] = rhs
    e1[m] = winv1 * rhs
    return left_0, left_1


def middle_left(m, f1, e1, east1, north1, upper1):
    return KEEP * f1[m] + around(e1, m, east1, north1, upper1, 2)


def hand_out(f2, e2, weights2, to_north, to_south):
    to_north[0], to_north[1] = f2[1], e2[0]
    to_south[0], to_south[1] = f2[0], e2[1]
    if to_north.shape[0] > 2:
        for j, kind in enumerate((0, 1, 3)):
            to_north[2 + j] = weights2[kind, 3]
            to_south[2 + j] = weights2[kind, 2]
        to_north[5] = weights2[2, 2]
        to_south[5] = weights2[2, 2]


def weigh(sets, share, width):
    level = lax.broadcasted_iota(jnp.int32, (LEV, width), 0)
    top = level == LEV - 1
    edge = top | (level == 0)

    def blend(column):
        sea = jnp.concatenate([sets[column]] * (width // 128), axis=1)
        return sea + share * jnp.concatenate([sets[column + 4]] * (width // 128), axis=1)

    lev_weight = blend(3)
    react = blend(0) + jnp.where(edge, 0.5 * lev_weight, 0.0)
    upper = jnp.where(top, 0.0, 0.5 * (lev_weight + next_level(lev_weight)))
    return react, upper, blend(1), blend(2)


def weigh_kernel(
    b_ref, x_ref, c_ref, from_north, from_south, sets,
    b, x, react, upper, lon_weight, lat_weight,
    share,
):
    share[...] = jnp.swapaxes(c_ref[...], 0, 1)
    b[RIM:RIM + ROWS] = jnp.swapaxes(b_ref[...], 0, 1)
    x[RIM:RIM + ROWS] = jnp.swapaxes(x_ref[...], 0, 1)

    def own(r):
        i = r + RIM
        react[i], upper[i], lon_weight[i], lat_weight[i] = weigh(sets, share[r], OWN)

    loop(0, ROWS, own)
    for i, b_row, x_row, c_row in outer_planes(from_north, from_south):
        if b_row is not None:
            b[i] = b_row
        x[i] = x_row
        react[i], upper[i], lon_weight[i], lat_weight[i] = weigh(sets, c_row, OWN)


class Joined:
    def __init__(self, main, rims):
        self.main, self.rims = main, rims

    def __getitem__(self, i):
        return jnp.concatenate([self.main[i], self.rims[i]], axis=1)


def first_down_kernel(
    b_main, x_main, react_main, upper_main, lon_main, lat_main, rim, rim_north, rim_south, sets, blocks,
    s, f2_out, to_north, to_south, weights2, e0, f1, e1, east, north, upper, winv, diag, east1, north1, upper1, winv1,
    b_rims, x_rims, react_rims, upper_rims, lon_rims, lat_rims, react, react1, stage,
):
    b, x, react_in = Joined(b_main, b_rims), Joined(x_main, x_rims), Joined(react_main, react_rims)
    upper_in, lon_weight, lat_weight = Joined(upper_main, upper_rims), Joined(lon_main, lon_rims), Joined(lat_main, lat_rims)
    lane = lane_ids()
    even = lane % 2 == 0
    lat = lax.axis_index("lat")
    south_end = lat == 0
    north_end = lat == lax.axis_size("lat") - 1

    rows = list(outer_planes(rim_north, rim_south))
    rows += [(RIM + r, rim[r, 0], rim[r, 1], rim[r, 2]) for r in range(ROWS)]
    for i, b_row, x_row, c_row in rows:
        if b_row is not None:
            b_rims[i] = b_row
        x_rims[i] = x_row
        react_rims[i], upper_rims[i], lon_rims[i], lat_rims[i] = weigh(sets, c_row, 128)

    def face_east(i):
        here = lon_weight[i]
        east[i] = 0.5 * (here + next_lane(here))
        upper[i] = upper_in[i]

    face_east(0)
    face_east(EXT - 1)

    def face(i):
        closed = (south_end & (i == RIM - 1)) | (north_end & (i == RIM + ROWS - 1))
        north[i] = jnp.where(closed, 0.0, 0.5) * (lat_weight[i] + lat_weight[i + 1])

    face(0)

    def start(i):
        face(i)
        face_east(i)
        at_end = (south_end & (i == RIM)) | (north_end & (i == RIM + ROWS - 1))
        whole = react_in[i] + jnp.where(at_end, 0.5, 0.0) * lat_weight[i]
        react[i] = whole
        whole = whole + east[i] + prev_lane(east[i]) + north[i] + north[i - 1]
        whole = whole + upper[i] + prev_level(upper[i])
        diag[i] = whole
        inverse = DAMP / whole
        winv[i] = inverse
        left = b[i] - (whole * x[i] - around(x, i, east, north, upper, 1))
        s[i] = left
        e0[i] = inverse * left

    loop(1, EXT - 1, start)

    north1[0] = 0.25 * pair_sum(north[1], even)

    def middle(m):
        i = 2 * m
        react1[m] = 0.25 * pair_sum(react[i] + react[i + 1], even)
        upper1[m] = 0.25 * pair_sum(upper[i] + upper[i + 1], even)
        eastern = east[i] + east[i + 1]
        east1[m] = 0.25 * jnp.where(even, next_lane(eastern), eastern)
        north1[m] = 0.25 * pair_sum(north[i + 1], even)
        whole = react1[m] + east1[m] + prev_lane(east1[m], 2) + north1[m] + north1[m - 1]
        inverse = DAMP / (whole + upper1[m] + prev_level(upper1[m]))
        winv1[m] = inverse
        restrict(m, s, e0, f1, e1, inverse, east, north, upper, even)

    loop(1, MID - 1, middle)

    last_of_four = lane % 4 == 3
    for c in range(2):
        m = 2 + 2 * c
        stage[c] = 0.125 * (react1[m] + react1[m + 1])
        stage[2 + c] = 0.125 * (upper1[m] + upper1[m + 1])
        stage[4 + c] = jnp.where(last_of_four, 0.25 * (east1[m] + east1[m + 1]), 0.0)
        left = middle_left(m, f1, e1, east1, north1, upper1)
        stage[6 + c] = 0.125 * (left + middle_left(m + 1, f1, e1, east1, north1, upper1))
    for c in range(3):
        stage[8 + c] = 0.125 * north1[1 + 2 * c]
    packed = times_blocks(stage[...].reshape(11 * LEV, LANES), blocks, 0).reshape(11, LEV, COLS)
    col = lax.broadcasted_iota(jnp.int32, (LEV, COLS), 1)
    empty = (col >= OWN_COLS + HALF_COLS) & (col < COLS - HALF_COLS)
    for c in range(2):
        upper2, east2, north2 = packed[2 + c], packed[4 + c], packed[9 + c]
        whole = packed[c] + east2 + prev_lane(east2) + north2 + packed[8 + c]
        whole = whole + upper2 + prev_level(upper2)
        weights2[0, 2 + c] = DAMP / jnp.where(empty, 1.0, whole)
        weights2[1, 2 + c] = east2
        weights2[2, 2 + c] = north2
        weights2[3, 2 + c] = upper2
    weights2[2, 1] = packed[8]
    f2 = (packed[6], packed[7])
    f2_out[0], f2_out[1] = f2
    hand_out(f2, (weights2[0, 2] * f2[0], weights2[0, 3] * f2[1]), weights2, to_north, to_south)


def sweep(k, f2, now, weights2):
    return KEEP * now[k] + weights2[0, k] * (
        f2[k] + around(now, k, weights2.at[1], weights2.at[2], weights2.at[3], 1)
    )


def two_sweeps(mine, north, south, weights2, f2, now, later):
    f2[1], f2[2], f2[3], f2[4] = south[0], mine[0], mine[1], north[0]
    now[0], now[5] = south[1], north[1]
    for k in range(1, 5):
        now[k] = weights2[0, k] * f2[k]
    for k in range(1, 5):
        later[k] = sweep(k, f2, now, weights2)
    return sweep(2, f2, later, weights2), sweep(3, f2, later, weights2)


def hand_on(e2, e1, to_north, to_south):
    for to, m in ((to_north, 4), (to_south, 3)):
        to[:, :COLS] = e2[0]
        to[:, COLS:2 * COLS] = e2[1]
        to[:, 2 * COLS:] = e1[m]


def coarse_kernel(mine, from_north, from_south, weights2, e1, f2, e2, to_north, to_south, whole2, now, later):
    for kind in range(4):
        for k in (2, 3):
            whole2[kind, k] = weights2[kind, k]
    for j, kind in enumerate((0, 1, 3)):
        whole2[kind, 1] = from_south[2 + j]
        whole2[kind, 4] = from_north[2 + j]
    whole2[2, 0], whole2[2, 1], whole2[2, 4] = from_south[5], weights2[2, 1], from_north[5]
    e2[0], e2[1] = two_sweeps(mine, from_north, from_south, whole2, f2, now, later)
    hand_on(e2, e1, to_north, to_south)


def coarse_dot_kernel(
    mine, from_north, from_south, weights2, e1, sums, sum_wq, f2, e2, to_north, to_south, dots, now, later
):
    e2[0], e2[1] = two_sweeps(mine, from_north, from_south, weights2, f2, now, later)
    hand_on(e2, e1, to_north, to_south)
    total = jnp.zeros((LEV, OWN_COLS), F32)
    for r in range(2):
        k = 2 + r
        first = now[k]
        once, twice = later[k], e2[r]
        term = f2[k] * once + (once - first) * (twice - first) / weights2[0, k]
        total = total + term[:, :OWN_COLS]
    column = lax.broadcasted_iota(jnp.int32, dots.shape, 1)
    line = jnp.where(column == 0, jnp.sum(sums[0]), 0.0) + jnp.where(column == 1, jnp.sum(sums[1]), 0.0)
    dots[...] = line + jnp.where(column == 2, jnp.sum(sum_wq[...]) + 16.0 * jnp.sum(total), 0.0)


def ascend(
    e2, from_north, from_south, f2, weights2, blocks, first, end, f, e0, f1, e1, winv, east, north, upper,
    winv1, east1, north1, upper1, now, sum1, sum0, result,
):
    for r in range(2):
        cols = slice(r * COLS, (r + 1) * COLS)
        now[r], now[2 + r], now[4 + r] = from_south[:, cols], e2[r], from_north[:, cols]
    rows = jnp.concatenate([sweep(k, f2, now, weights2) for k in range(1, 5)], axis=0)
    wide = times_blocks(rows, blocks, 1).reshape(4, LEV, LANES)
    for m in range(1, MID - 1):
        sum1[m] = e1[m] + wide[m // 2]
    sum1[0] = from_south[:, 2 * COLS:] + wide[0]
    sum1[MID - 1] = from_north[:, 2 * COLS:] + wide[3]

    def middle(m):
        better = KEEP * sum1[m] + winv1[m] * (f1[m] + around(sum1, m, east1, north1, upper1, 2))
        sum0[2 * m] = e0[2 * m] + better
        sum0[2 * m + 1] = e0[2 * m + 1] + better

    loop(1, MID - 1, middle)

    def fine(i):
        result[i] = KEEP * sum0[i] + winv[i] * (f[i] + around(sum0, i, east, north, upper, 1))

    loop(first, end, fine)


def first_up_kernel(
    e2, from_north, from_south, f2, weights2, blocks,
    s, e0, f1, e1, winv, east, north, upper, winv1, east1, north1, upper1, diag,
    p_own, w_own, w_north, w_south, s_own, sums,
    now, sum1, sum0, p,
):
    ascend(
        e2, from_north, from_south, f2, weights2, blocks, RIM - 1, RIM + ROWS + 1, s, e0, f1, e1, winv, east, north, upper,
        winv1, east1, north1, upper1, now, sum1, sum0, p,
    )

    def image(r, totals):
        i = r + RIM
        w_row = diag[i] * p[i] - around(p, i, east, north, upper, 1)
        w_own[r] = w_row
        p_row, s_row = p[i, :, :OWN], s[i, :, :OWN]
        p_own[r] = p_row
        s_own[r] = s_row
        return totals[0] + s_row * p_row, totals[1] + p_row * w_row[:, :OWN]

    zero = jnp.zeros((LEV, OWN), F32)
    sums[0], sums[1] = lax.fori_loop(0, ROWS, image, (zero, zero), unroll=True)
    w_south[...] = w_own[:SEND]
    w_north[...] = w_own[ROWS - SEND:]


def second_down_kernel(
    w_own, from_north, from_south, weights2, blocks, winv, east, north, upper, winv1, east1, north1, upper1,
    f2_out, to_north, to_south, e0, f1, e1, sum_wq,
    w, stage,
):
    even = lane_ids() % 2 == 0
    w[RIM - SEND:RIM] = from_south[...]
    w[RIM + ROWS:RIM + ROWS + SEND] = from_north[...]
    for r in range(ROWS):
        w[RIM + r] = w_own[r]

    def smooth(i):
        e0[i] = winv[i] * w[i]

    loop(1, EXT - 1, smooth)

    def down(m):
        return restrict(m, w, e0, f1, e1, winv1[m], east, north, upper, even)

    down(1)
    down(MID - 2)

    def down_own(m, total):
        left_0, left_1 = down(m)
        i = 2 * m
        term = e0[i] * (w[i] + left_0) + e0[i + 1] * (w[i + 1] + left_1)
        return total + term[:, :OWN]

    total = lax.fori_loop(2, 6, down_own, jnp.zeros((LEV, OWN), F32), unroll=4)
    for c in range(2):
        pair = 0.0
        for m in (2 + 2 * c, 3 + 2 * c):
            left = middle_left(m, f1, e1, east1, north1, upper1)
            total = total + 2.0 * (e1[m] * (f1[m] + left))[:, :OWN]
            pair = pair + left
        stage[c] = 0.125 * pair
    sum_wq[...] = total
    packed = times_blocks(stage[...].reshape(2 * LEV, LANES), blocks, 0).reshape(2, LEV, COLS)
    f2 = (packed[0], packed[1])
    f2_out[0], f2_out[1] = f2
    hand_out(f2, (weights2[0, 2] * f2[0], weights2[0, 3] * f2[1]), weights2, to_north, to_south)


def second_up_kernel(
    e2, from_north, from_south, f2, weights2, blocks,
    w_own, e0, f1, e1, winv, east, north, upper, winv1, east1, north1, upper1, dots,
    q_out, dots_out,
    now, sum1, sum0, w, result,
):
    for r in range(ROWS):
        w[RIM + r] = w_own[r]
    ascend(
        e2, from_north, from_south, f2, weights2, blocks, RIM, RIM + ROWS, w, e0, f1, e1, winv, east, north, upper,
        winv1, east1, north1, upper1, now, sum1, sum0, result,
    )
    dots_out[...] = dots[...]
    q_out[...] = jnp.swapaxes(result[RIM:RIM + ROWS, :, :OWN], 0, 1)


def turn_kernel(p, w, s, p_out, w_out, s_out):
    p_out[...] = jnp.swapaxes(p[...], 0, 1)
    w_out[...] = jnp.swapaxes(w[:, :, :OWN], 0, 1)
    s_out[...] = jnp.swapaxes(s[...], 0, 1)


def total_kernel(lines, total):
    total[...] = jnp.broadcast_to(jnp.sum(lines[...], axis=0, keepdims=True), total.shape)


def finish_kernel(dots, x, p, w, q, s, iterate, residual, direction):
    line = jnp.sum(dots[...], axis=0, keepdims=True)
    column = lax.broadcasted_iota(jnp.int32, (1, 128), 1)
    sp, pw, wq = [jnp.sum(jnp.where(column == j, line, 0.0), axis=1, keepdims=True)[None] for j in range(3)]
    step = sp / pw
    next_dot = (sp - step * pw) - step * (pw - step * wq)
    ratio = next_dot / sp
    iterate[...] = x[...] + step * p[...]
    residual[...] = s[...] - step * w[...]
    direction[...] = (p[...] - step * q[...]) + ratio * p[...]


def shards(right_side, initial_guess, land_mask, coefficient_sets):
    z_size, lat_size = lax.axis_size("z"), lax.axis_size("lat")
    lines = (lax.axis_size("x") * lat_size, 128)
    lon = ("x", "z")
    sizes = {lon: lax.axis_size("x") * z_size, "lat": lat_size}

    def trade(to_next, to_last, axis):
        size = sizes[axis]
        up = [(i, (i + 1) % size) for i in range(size)]
        from_last = lax.ppermute(to_next, axis, up)
        return lax.ppermute(to_last, axis, [(j, i) for i, j in up]), from_last

    row, fine, mid, line = (LEV, LANES), (EXT, LEV, LANES), (MID, LEV, LANES), (LEV, COLS)
    fields = [right_side, initial_guess, land_mask]
    blocks = blocks_matrix()
    to_north, to_south, to_east, to_west = call(
        pack_kernel,
        [(PLANES, LEV, OWN)] * 2 + [(ROWS, LEV, 128)] * 2,
        fields,
        [(3, LEV, ROWS, OWN), (3, ROWS, LEV, 256)] + [(PLANES, LEV, OWN)] * 2 + [(ROWS, LEV, 128)] * 2,
        specs=[HBM] * 3,
        copies=7,
        out_spec=HBM,
    )
    lat_rows = trade(to_north, to_south, "lat")
    lon_rims = trade(to_east, to_west, lon)
    rim, to_north, to_south = call(
        rim_kernel, [(ROWS, 3, LEV, 128), (PLANES, LEV, 128), (PLANES, LEV, 128)], lon_rims
    )
    lat_rims = trade(to_north, to_south, "lat")
    sea, land = coefficient_sets[0], coefficient_sets[1]
    sets = jnp.broadcast_to(jnp.concatenate([sea, land - sea])[:, :, None], (8, LEV, 128))

    main, side = (EXT, LEV, OWN), (EXT, LEV, 128)
    weighed = call(weigh_kernel, [main] * 6, fields + [*lat_rows, sets], [(ROWS, LEV, OWN)])
    (s, f2, to_north, to_south, weights2, e0, f1, e1, east, north, upper, winv, diag, east1, north1, upper1, winv1) = call(
        first_down_kernel,
        [fine, (2,) + line, (6,) + line, (6,) + line, (4, NEAR) + line, fine, mid, mid, fine, fine, fine, fine, fine, mid, mid, mid, mid],
        [*weighed, rim, *lat_rims, sets, blocks],
        [side] * 6 + [fine, mid, (11,) + row],
    )
    grids = [winv, east, north, upper, winv1, east1, north1, upper1]
    near = (NEAR,) + line
    edge = (LEV, 2 * COLS + LANES)
    f2_near, e2, edge_north, edge_south, weights2 = call(
        coarse_kernel,
        [near, (2,) + line, edge, edge, (4, NEAR) + line],
        [f2, *trade(to_north, to_south, "lat"), weights2, e1],
        [near, near],
    )
    p_own, w_own, to_north, to_south, s_own, sums = call(
        first_up_kernel,
        [(ROWS, LEV, OWN), (ROWS,) + row, (SEND,) + row, (SEND,) + row, (ROWS, LEV, OWN), (2, LEV, OWN)],
        [e2, *trade(edge_north, edge_south, "lat"), f2_near, weights2, blocks, s, e0, f1, e1] + grids + [diag],
        [near, mid, fine, fine],
    )
    w_rows = trade(to_north, to_south, "lat")
    p, w, s = call(turn_kernel, [(LEV, ROWS, OWN)] * 3, [p_own, w_own, s_own])
    f2, to_north, to_south, e0, f1, e1, sum_wq = call(
        second_down_kernel,
        [(2,) + line] * 3 + [fine, mid, mid, (LEV, OWN)],
        [w_own, *w_rows, weights2, blocks] + grids,
        [fine, (2,) + row],
    )
    f2_near, e2, edge_north, edge_south, dots = call(
        coarse_dot_kernel,
        [near, (2,) + line, edge, edge, lines],
        [f2, *trade(to_north, to_south, "lat"), weights2, e1, sums, sum_wq],
        [near, near],
    )
    q, dots = call(
        second_up_kernel,
        [(LEV, ROWS, OWN), lines],
        [e2, *trade(edge_north, edge_south, "lat"), f2_near, weights2, blocks, w_own, e0, f1, e1] + grids + [dots],
        [near, mid, fine, fine, fine],
    )
    (dots,) = call(total_kernel, [(z_size, 128)], [lax.all_to_all(dots, ("x", "lat"), 0, 0, tiled=True)])
    dots = lax.all_to_all(dots, "z", 0, 0, tiled=True)
    return tuple(call(finish_kernel, [(LEV, ROWS, OWN)] * 3, [dots, initial_guess, p, w, q, s]))


def solution(mesh):
    lon, lat = mesh.shape["lon"], mesh.shape["lat"]
    z = 16 if lon % 16 == 0 else lon
    grid = jax.sharding.Mesh(mesh.devices.reshape(lon // z, z, lat), ("x", "z", "lat"))
    field = P(None, "lat", ("x", "z"))
    return jax.shard_map(
        shards, mesh=grid, in_specs=(field, field, field, P()), out_specs=(field, field, field), check_vma=False
    )
```

```python
import jax
import jax.numpy as jnp
import numpy as np
from jax import lax
from jax.experimental import pallas as pl
from jax.experimental.pallas import tpu as pltpu
from jax.sharding import PartitionSpec as P


LEV = 16
ROWS = 8
OWN = 512
HALF = 64
DEEP = 42
LANES = OWN + 2 * HALF
RIM = 4
EXT = ROWS + 2 * RIM
MID = EXT // 2
SEND = 3
NEAR = 6
COLS = 256
OWN_COLS = OWN // 4
HALF_COLS = HALF // 4
DAMP = 0.8
KEEP = 1.0 - DAMP
F32 = jnp.float32

VMEM = pl.BlockSpec(memory_space=pltpu.VMEM)
HBM = pl.BlockSpec(memory_space=pltpu.HBM)


def call(body, outs, ins, scratch=(), specs=(), copies=0, out_spec=VMEM):
    return pl.pallas_call(
        body,
        out_shape=[jax.ShapeDtypeStruct(o, F32) for o in outs],
        in_specs=list(specs) + [VMEM] * (len(ins) - len(specs)),
        out_specs=[out_spec] * len(outs),
        scratch_shapes=[pltpu.VMEM(s, F32) for s in scratch] + [pltpu.SemaphoreType.DMA((copies,))] * (copies > 0),
        compiler_params=pltpu.CompilerParams(vmem_limit_bytes=(60 if copies else 24) * 1024 * 1024),
        cost_estimate=pl.CostEstimate(flops=1000000, bytes_accessed=1000000, transcendentals=0),
    )(*ins)


def loop(first, end, body):
    def step(i, carry):
        body(i)
        return carry

    lax.fori_loop(first, end, step, 0, unroll=True)


def lane_ids():
    return lax.broadcasted_iota(jnp.int32, (LEV, LANES), 1)


def next_lane(v, n=1):
    return pltpu.roll(v, v.shape[-1] - n, axis=1)


def prev_lane(v, n=1):
    return pltpu.roll(v, n, axis=1)


def next_level(v):
    return pltpu.roll(v, LEV - 1, axis=0)


def prev_level(v):
    return pltpu.roll(v, 1, axis=0)


def pair_sum(v, even):
    return v + jnp.where(even, next_lane(v), prev_lane(v))


def around(v, i, east, north, upper, n):
    here = v[i]
    total = east[i] * next_lane(here, n) + prev_lane(east[i] * here, n)
    total = total + upper[i] * next_level(here) + prev_level(upper[i] * here)
    return total + north[i] * v[i + 1] + north[i - 1] * v[i - 1]


def blocks_matrix():
    lane = np.arange(LANES)
    cell = lane // 4
    cell = np.where(cell < OWN_COLS + HALF_COLS, cell, cell + COLS - LANES // 4)
    matrix = np.zeros((LANES, COLS), np.float32)
    matrix[lane, cell] = 1.0
    return jnp.asarray(matrix, jnp.bfloat16)


def times_blocks(rows, blocks, side):
    total = 0.0
    left = rows
    for _ in range(3):
        part = left.astype(jnp.bfloat16)
        left = left - part.astype(F32)
        total = total + lax.dot_general(part, blocks[...], (((1,), (side,)), ((), ())), preferred_element_type=F32)
    return total


def pack_kernel(
    b_ref, x_ref, c_ref, to_north, to_south, to_east, to_west,
    held, turned, north_ref, south_ref, east_ref, west_ref, moved,
):
    lane = lax.broadcasted_iota(jnp.int32, (LEV, 128), 1)
    copies = [pltpu.make_async_copy(ref, held.at[j], moved.at[j]) for j, ref in enumerate((b_ref, x_ref, c_ref))]
    for copy in copies:
        copy.start()
    for j, copy in enumerate(copies):
        copy.wait()
        field = jnp.swapaxes(held[j], 0, 1)
        turned[j, :, :, :128] = field[:, :, :128]
        turned[j, :, :, 128:] = field[:, :, OWN - 128:]
        south_ref[:, j] = field[:RIM]
        north_ref[:, j] = field[ROWS - RIM:]
    results = ((north_ref, to_north), (south_ref, to_south), (east_ref, to_east), (west_ref, to_west))
    copies = [pltpu.make_async_copy(a, b, moved.at[3 + j]) for j, (a, b) in enumerate(results)]
    copies[0].start()
    copies[1].start()
    for r in range(ROWS):
        b, x, c = [turned[j, r, :, :128] for j in range(3)]
        west_ref[r] = jnp.where(lane < DEEP, b, jnp.where(lane < 2 * DEEP, prev_lane(x, DEEP), prev_lane(c, 2 * DEEP)))
        b, x, c = [turned[j, r, :, 128:] for j in range(3)]
        x, c = next_lane(x, DEEP), next_lane(c, 2 * DEEP)
        east_ref[r] = jnp.where(lane >= 128 - DEEP, b, jnp.where(lane >= 128 - 2 * DEEP, x, c))
    copies[2].start()
    copies[3].start()
    for copy in copies:
        copy.wait()


def rim_kernel(from_east, from_west, rim_ref, north_ref, south_ref):
    lane = lax.broadcasted_iota(jnp.int32, (LEV, 128), 1)
    for r in range(ROWS):
        east, west = from_east[r], from_west[r]
        for j in range(3):
            if j > 0:
                east, west = next_lane(east, DEEP), prev_lane(west, DEEP)
            rim_ref[r, j] = jnp.where(lane < DEEP, east, jnp.where(lane >= 128 - DEEP, west, 0.0))
    south_ref[...] = rim_ref[:RIM]
    north_ref[...] = rim_ref[ROWS - RIM:]


def restrict(m, f, e0, f1, e1, winv1, east, north, upper, even):
    i = 2 * m
    left_0 = KEEP * f[i] + around(e0, i, east, north, upper, 1)
    left_1 = KEEP * f[i + 1] + around(e0, i + 1, east, north, upper, 1)
    rhs = 0.25 * pair_sum(left_0 + left_1, even)
    f1[m] = rhs
    e1[m] = winv1 * rhs
    return left_0, left_1


def middle_left(m, f1, e1, east1, north1, upper1):
    return KEEP * f1[m] + around(e1, m, east1, north1, upper1, 2)


def hand_out(f2, e2, weights2, to_north, to_south):
    to_north[0], to_north[1] = f2[1], e2[0]
    to_south[0], to_south[1] = f2[0], e2[1]
    if to_north.shape[0] > 2:
        for j, kind in enumerate((0, 1, 3)):
            to_north[2 + j] = weights2[kind, 3]
            to_south[2 + j] = weights2[kind, 2]
        to_north[5] = weights2[2, 2]
        to_south[5] = weights2[2, 2]


def weigh(sets, share, width):
    level = lax.broadcasted_iota(jnp.int32, (LEV, width), 0)
    top = level == LEV - 1
    edge = top | (level == 0)

    def blend(column):
        sea = jnp.concatenate([sets[column]] * (width // 128), axis=1)
        return sea + share * jnp.concatenate([sets[column + 4]] * (width // 128), axis=1)

    lev_weight = blend(3)
    react = blend(0) + jnp.where(edge, 0.5 * lev_weight, 0.0)
    upper = jnp.where(top, 0.0, 0.5 * (lev_weight + next_level(lev_weight)))
    return react, upper, blend(1), blend(2)


def weigh_kernel(
    b_ref, x_ref, c_ref, from_north, from_south, sets,
    b, x, react, upper, lon_weight, lat_weight,
    share,
):
    share[...] = jnp.swapaxes(c_ref[...], 0, 1)
    b[RIM:RIM + ROWS] = jnp.swapaxes(b_ref[...], 0, 1)
    x[RIM:RIM + ROWS] = jnp.swapaxes(x_ref[...], 0, 1)

    def own(r):
        i = r + RIM
        react[i], upper[i], lon_weight[i], lat_weight[i] = weigh(sets, share[r], OWN)

    def outer(i, rows, r):
        b[i] = rows[r, 0]
        x[i] = rows[r, 1]
        react[i], upper[i], lon_weight[i], lat_weight[i] = weigh(sets, rows[r, 2], OWN)

    loop(0, ROWS, own)
    loop(0, RIM, lambda r: outer(r, from_south, r))
    loop(0, RIM, lambda r: outer(r + RIM + ROWS, from_north, r))


class Joined:
    def __init__(self, main, rims):
        self.main, self.rims = main, rims

    def __getitem__(self, i):
        return jnp.concatenate([self.main[i], self.rims[i]], axis=1)


def first_down_kernel(
    b_main, x_main, react_main, upper_main, lon_main, lat_main, rim, rim_north, rim_south, sets, blocks,
    s, f2_out, to_north, to_south, weights2, e0, f1, e1, east, north, upper, winv, diag, east1, north1, upper1, winv1,
    b_rims, x_rims, react_rims, upper_rims, lon_rims, lat_rims, react, react1, stage,
):
    b, x, react_in = Joined(b_main, b_rims), Joined(x_main, x_rims), Joined(react_main, react_rims)
    upper_in, lon_weight, lat_weight = Joined(upper_main, upper_rims), Joined(lon_main, lon_rims), Joined(lat_main, lat_rims)
    lane = lane_ids()
    even = lane % 2 == 0
    lat = lax.axis_index("lat")
    south_end = lat == 0
    north_end = lat == lax.axis_size("lat") - 1

    def take(i, rows, r):
        b_rims[i] = rows[r, 0]
        x_rims[i] = rows[r, 1]
        react_rims[i], upper_rims[i], lon_rims[i], lat_rims[i] = weigh(sets, rows[r, 2], 128)

    for r in range(RIM):
        take(r, rim_south, r)
        take(r + RIM + ROWS, rim_north, r)
    for r in range(ROWS):
        take(r + RIM, rim, r)

    def face_east(i):
        here = lon_weight[i]
        east[i] = 0.5 * (here + next_lane(here))
        upper[i] = upper_in[i]

    face_east(0)
    face_east(EXT - 1)

    def face(i):
        closed = (south_end & (i == RIM - 1)) | (north_end & (i == RIM + ROWS - 1))
        north[i] = jnp.where(closed, 0.0, 0.5) * (lat_weight[i] + lat_weight[i + 1])

    face(0)

    def start(i):
        face(i)
        face_east(i)
        at_end = (south_end & (i == RIM)) | (north_end & (i == RIM + ROWS - 1))
        whole = react_in[i] + jnp.where(at_end, 0.5, 0.0) * lat_weight[i]
        react[i] = whole
        whole = whole + east[i] + prev_lane(east[i]) + north[i] + north[i - 1]
        whole = whole + upper[i] + prev_level(upper[i])
        diag[i] = whole
        inverse = DAMP / whole
        winv[i] = inverse
        left = b[i] - (whole * x[i] - around(x, i, east, north, upper, 1))
        s[i] = left
        e0[i] = inverse * left

    loop(1, EXT - 1, start)

    north1[0] = 0.25 * pair_sum(north[1], even)

    def middle(m):
        i = 2 * m
        react1[m] = 0.25 * pair_sum(react[i] + react[i + 1], even)
        upper1[m] = 0.25 * pair_sum(upper[i] + upper[i + 1], even)
        eastern = east[i] + east[i + 1]
        east1[m] = 0.25 * jnp.where(even, next_lane(eastern), eastern)
        north1[m] = 0.25 * pair_sum(north[i + 1], even)
        whole = react1[m] + east1[m] + prev_lane(east1[m], 2) + north1[m] + north1[m - 1]
        inverse = DAMP / (whole + upper1[m] + prev_level(upper1[m]))
        winv1[m] = inverse
        restrict(m, s, e0, f1, e1, inverse, east, north, upper, even)

    loop(1, MID - 1, middle)

    last_of_four = lane % 4 == 3
    for c in range(2):
        m = 2 + 2 * c
        stage[c] = 0.125 * (react1[m] + react1[m + 1])
        stage[2 + c] = 0.125 * (upper1[m] + upper1[m + 1])
        stage[4 + c] = jnp.where(last_of_four, 0.25 * (east1[m] + east1[m + 1]), 0.0)
        left = middle_left(m, f1, e1, east1, north1, upper1)
        stage[6 + c] = 0.125 * (left + middle_left(m + 1, f1, e1, east1, north1, upper1))
    for c in range(3):
        stage[8 + c] = 0.125 * north1[1 + 2 * c]
    packed = times_blocks(stage[...].reshape(11 * LEV, LANES), blocks, 0).reshape(11, LEV, COLS)
    col = lax.broadcasted_iota(jnp.int32, (LEV, COLS), 1)
    empty = (col >= OWN_COLS + HALF_COLS) & (col < COLS - HALF_COLS)
    for c in range(2):
        upper2, east2, north2 = packed[2 + c], packed[4 + c], packed[9 + c]
        whole = packed[c] + east2 + prev_lane(east2) + north2 + packed[8 + c]
        whole = whole + upper2 + prev_level(upper2)
        weights2[0, 2 + c] = DAMP / jnp.where(empty, 1.0, whole)
        weights2[1, 2 + c] = east2
        weights2[2, 2 + c] = north2
        weights2[3, 2 + c] = upper2
    weights2[2, 1] = packed[8]
    f2 = (packed[6], packed[7])
    f2_out[0], f2_out[1] = f2
    hand_out(f2, (weights2[0, 2] * f2[0], weights2[0, 3] * f2[1]), weights2, to_north, to_south)


def sweep(k, f2, now, weights2):
    return KEEP * now[k] + weights2[0, k] * (
        f2[k] + around(now, k, weights2.at[1], weights2.at[2], weights2.at[3], 1)
    )


def two_sweeps(mine, north, south, weights2, f2, now, later):
    f2[1], f2[2], f2[3], f2[4] = south[0], mine[0], mine[1], north[0]
    now[0], now[5] = south[1], north[1]
    for k in range(1, 5):
        now[k] = weights2[0, k] * f2[k]
    for k in range(1, 5):
        later[k] = sweep(k, f2, now, weights2)
    return sweep(2, f2, later, weights2), sweep(3, f2, later, weights2)


def hand_on(e2, e1, to_north, to_south):
    for to, m in ((to_north, 4), (to_south, 3)):
        to[:, :COLS] = e2[0]
        to[:, COLS:2 * COLS] = e2[1]
        to[:, 2 * COLS:] = e1[m]


def coarse_kernel(mine, from_north, from_south, weights2, e1, f2, e2, to_north, to_south, whole2, now, later):
    for kind in range(4):
        for k in (2, 3):
            whole2[kind, k] = weights2[kind, k]
    for j, kind in enumerate((0, 1, 3)):
        whole2[kind, 1] = from_south[2 + j]
        whole2[kind, 4] = from_north[2 + j]
    whole2[2, 0], whole2[2, 1], whole2[2, 4] = from_south[5], weights2[2, 1], from_north[5]
    e2[0], e2[1] = two_sweeps(mine, from_north, from_south, whole2, f2, now, later)
    hand_on(e2, e1, to_north, to_south)


def coarse_dot_kernel(
    mine, from_north, from_south, weights2, e1, sums, sum_wq, f2, e2, to_north, to_south, dots, now, later
):
    e2[0], e2[1] = two_sweeps(mine, from_north, from_south, weights2, f2, now, later)
    hand_on(e2, e1, to_north, to_south)
    total = jnp.zeros((LEV, OWN_COLS), F32)
    for r in range(2):
        k = 2 + r
        first = now[k]
        once, twice = later[k], e2[r]
        term = f2[k] * once + (once - first) * (twice - first) / weights2[0, k]
        total = total + term[:, :OWN_COLS]
    column = lax.broadcasted_iota(jnp.int32, dots.shape, 1)
    line = jnp.where(column == 0, jnp.sum(sums[0]), 0.0) + jnp.where(column == 1, jnp.sum(sums[1]), 0.0)
    dots[...] = line + jnp.where(column == 2, jnp.sum(sum_wq[...]) + 16.0 * jnp.sum(total), 0.0)


def ascend(
    e2, from_north, from_south, f2, weights2, blocks, first, end, f, e0, f1, e1, winv, east, north, upper,
    winv1, east1, north1, upper1, now, sum1, sum0, result,
):
    for r in range(2):
        cols = slice(r * COLS, (r + 1) * COLS)
        now[r], now[2 + r], now[4 + r] = from_south[:, cols], e2[r], from_north[:, cols]
    rows = jnp.concatenate([sweep(k, f2, now, weights2) for k in range(1, 5)], axis=0)
    wide = times_blocks(rows, blocks, 1).reshape(4, LEV, LANES)
    for m in range(1, MID - 1):
        sum1[m] = e1[m] + wide[m // 2]
    sum1[0] = from_south[:, 2 * COLS:] + wide[0]
    sum1[MID - 1] = from_north[:, 2 * COLS:] + wide[3]

    def middle(m):
        better = KEEP * sum1[m] + winv1[m] * (f1[m] + around(sum1, m, east1, north1, upper1, 2))
        sum0[2 * m] = e0[2 * m] + better
        sum0[2 * m + 1] = e0[2 * m + 1] + better

    loop(1, MID - 1, middle)

    def fine(i):
        result[i] = KEEP * sum0[i] + winv[i] * (f[i] + around(sum0, i, east, north, upper, 1))

    loop(first, end, fine)


def first_up_kernel(
    e2, from_north, from_south, f2, weights2, blocks,
    s, e0, f1, e1, winv, east, north, upper, winv1, east1, north1, upper1, diag,
    p_own, w_own, w_north, w_south, s_own, sums,
    now, sum1, sum0, p,
):
    ascend(
        e2, from_north, from_south, f2, weights2, blocks, RIM - 1, RIM + ROWS + 1, s, e0, f1, e1, winv, east, north, upper,
        winv1, east1, north1, upper1, now, sum1, sum0, p,
    )

    def image(r, totals):
        i = r + RIM
        w_row = diag[i] * p[i] - around(p, i, east, north, upper, 1)
        w_own[r] = w_row
        p_row, s_row = p[i, :, :OWN], s[i, :, :OWN]
        p_own[r] = p_row
        s_own[r] = s_row
        return totals[0] + s_row * p_row, totals[1] + p_row * w_row[:, :OWN]

    zero = jnp.zeros((LEV, OWN), F32)
    sums[0], sums[1] = lax.fori_loop(0, ROWS, image, (zero, zero), unroll=True)
    w_south[...] = w_own[:SEND]
    w_north[...] = w_own[ROWS - SEND:]


def second_down_kernel(
    w_own, from_north, from_south, weights2, blocks, winv, east, north, upper, winv1, east1, north1, upper1,
    f2_out, to_north, to_south, e0, f1, e1, sum_wq,
    w, stage,
):
    even = lane_ids() % 2 == 0
    w[RIM - SEND:RIM] = from_south[...]
    w[RIM + ROWS:RIM + ROWS + SEND] = from_north[...]
    for r in range(ROWS):
        w[RIM + r] = w_own[r]

    def smooth(i):
        e0[i] = winv[i] * w[i]

    loop(1, EXT - 1, smooth)

    def down(m):
        return restrict(m, w, e0, f1, e1, winv1[m], east, north, upper, even)

    down(1)
    down(MID - 2)

    def down_own(m, total):
        left_0, left_1 = down(m)
        i = 2 * m
        term = e0[i] * (w[i] + left_0) + e0[i + 1] * (w[i + 1] + left_1)
        return total + term[:, :OWN]

    total = lax.fori_loop(2, 6, down_own, jnp.zeros((LEV, OWN), F32), unroll=4)
    for c in range(2):
        pair = 0.0
        for m in (2 + 2 * c, 3 + 2 * c):
            left = middle_left(m, f1, e1, east1, north1, upper1)
            total = total + 2.0 * (e1[m] * (f1[m] + left))[:, :OWN]
            pair = pair + left
        stage[c] = 0.125 * pair
    sum_wq[...] = total
    packed = times_blocks(stage[...].reshape(2 * LEV, LANES), blocks, 0).reshape(2, LEV, COLS)
    f2 = (packed[0], packed[1])
    f2_out[0], f2_out[1] = f2
    hand_out(f2, (weights2[0, 2] * f2[0], weights2[0, 3] * f2[1]), weights2, to_north, to_south)


def second_up_kernel(
    e2, from_north, from_south, f2, weights2, blocks,
    w_own, e0, f1, e1, winv, east, north, upper, winv1, east1, north1, upper1, dots,
    q_out, dots_out,
    now, sum1, sum0, w, result,
):
    for r in range(ROWS):
        w[RIM + r] = w_own[r]
    ascend(
        e2, from_north, from_south, f2, weights2, blocks, RIM, RIM + ROWS, w, e0, f1, e1, winv, east, north, upper,
        winv1, east1, north1, upper1, now, sum1, sum0, result,
    )
    dots_out[...] = dots[...]
    q_out[...] = jnp.swapaxes(result[RIM:RIM + ROWS, :, :OWN], 0, 1)


def turn_kernel(p, w, s, p_out, w_out, s_out):
    p_out[...] = jnp.swapaxes(p[...], 0, 1)
    w_out[...] = jnp.swapaxes(w[:, :, :OWN], 0, 1)
    s_out[...] = jnp.swapaxes(s[...], 0, 1)


def total_kernel(lines, total):
    total[...] = jnp.broadcast_to(jnp.sum(lines[...], axis=0, keepdims=True), total.shape)


def finish_kernel(dots, x, p, w, q, s, iterate, residual, direction):
    line = jnp.sum(dots[...], axis=0, keepdims=True)
    column = lax.broadcasted_iota(jnp.int32, (1, 128), 1)
    sp, pw, wq = [jnp.sum(jnp.where(column == j, line, 0.0), axis=1, keepdims=True)[None] for j in range(3)]
    step = sp / pw
    next_dot = (sp - step * pw) - step * (pw - step * wq)
    ratio = next_dot / sp
    iterate[...] = x[...] + step * p[...]
    residual[...] = s[...] - step * w[...]
    direction[...] = (p[...] - step * q[...]) + ratio * p[...]


def shards(right_side, initial_guess, land_mask, coefficient_sets):
    z_size, lat_size = lax.axis_size("z"), lax.axis_size("lat")
    lines = (z_size, 128)
    lon = ("x", "z")
    sizes = {lon: lax.axis_size("x") * z_size, "lat": lat_size}

    def trade(to_next, to_last, axis):
        size = sizes[axis]
        up = [(i, (i + 1) % size) for i in range(size)]
        from_last = lax.ppermute(to_next, axis, up)
        return lax.ppermute(to_last, axis, [(j, i) for i, j in up]), from_last

    row, fine, mid, line = (LEV, LANES), (EXT, LEV, LANES), (MID, LEV, LANES), (LEV, COLS)
    fields = [right_side, initial_guess, land_mask]
    blocks = blocks_matrix()
    to_north, to_south, to_east, to_west = call(
        pack_kernel,
        [(RIM, 3, LEV, OWN)] * 2 + [(ROWS, LEV, 128)] * 2,
        fields,
        [(3, LEV, ROWS, OWN), (3, ROWS, LEV, 256)] + [(RIM, 3, LEV, OWN)] * 2 + [(ROWS, LEV, 128)] * 2,
        specs=[HBM] * 3,
        copies=7,
        out_spec=HBM,
    )
    lat_rows = trade(to_north, to_south, "lat")
    lon_rims = trade(to_east, to_west, lon)
    rim, to_north, to_south = call(
        rim_kernel, [(ROWS, 3, LEV, 128), (RIM, 3, LEV, 128), (RIM, 3, LEV, 128)], lon_rims
    )
    lat_rims = trade(to_north, to_south, "lat")
    sea, land = coefficient_sets[0], coefficient_sets[1]
    sets = jnp.broadcast_to(jnp.concatenate([sea, land - sea])[:, :, None], (8, LEV, 128))

    main, side = (EXT, LEV, OWN), (EXT, LEV, 128)
    weighed = call(weigh_kernel, [main] * 6, fields + [*lat_rows, sets], [(ROWS, LEV, OWN)])
    (s, f2, to_north, to_south, weights2, e0, f1, e1, east, north, upper, winv, diag, east1, north1, upper1, winv1) = call(
        first_down_kernel,
        [fine, (2,) + line, (6,) + line, (6,) + line, (4, NEAR) + line, fine, mid, mid, fine, fine, fine, fine, fine, mid, mid, mid, mid],
        [*weighed, rim, *lat_rims, sets, blocks],
        [side] * 6 + [fine, mid, (11,) + row],
    )
    grids = [winv, east, north, upper, winv1, east1, north1, upper1]
    near = (NEAR,) + line
    edge = (LEV, 2 * COLS + LANES)
    f2_near, e2, edge_north, edge_south, weights2 = call(
        coarse_kernel,
        [near, (2,) + line, edge, edge, (4, NEAR) + line],
        [f2, *trade(to_north, to_south, "lat"), weights2, e1],
        [near, near],
    )
    p_own, w_own, to_north, to_south, s_own, sums = call(
        first_up_kernel,
        [(ROWS, LEV, OWN), (ROWS,) + row, (SEND,) + row, (SEND,) + row, (ROWS, LEV, OWN), (2, LEV, OWN)],
        [e2, *trade(edge_north, edge_south, "lat"), f2_near, weights2, blocks, s, e0, f1, e1] + grids + [diag],
        [near, mid, fine, fine],
    )
    w_rows = trade(to_north, to_south, "lat")
    p, w, s = call(turn_kernel, [(LEV, ROWS, OWN)] * 3, [p_own, w_own, s_own])
    f2, to_north, to_south, e0, f1, e1, sum_wq = call(
        second_down_kernel,
        [(2,) + line] * 3 + [fine, mid, mid, (LEV, OWN)],
        [w_own, *w_rows, weights2, blocks] + grids,
        [fine, (2,) + row],
    )
    f2_near, e2, edge_north, edge_south, dots = call(
        coarse_dot_kernel,
        [near, (2,) + line, edge, edge, lines],
        [f2, *trade(to_north, to_south, "lat"), weights2, e1, sums, sum_wq],
        [near, near],
    )
    q, dots = call(
        second_up_kernel,
        [(LEV, ROWS, OWN), lines],
        [e2, *trade(edge_north, edge_south, "lat"), f2_near, weights2, blocks, w_own, e0, f1, e1] + grids + [dots],
        [near, mid, fine, fine, fine],
    )
    (dots,) = call(total_kernel, [(lax.axis_size("x") * lat_size, 128)], [lax.all_to_all(dots, "z", 0, 0, tiled=True)])
    dots = lax.all_to_all(dots, ("x", "lat"), 0, 0, tiled=True)
    return tuple(call(finish_kernel, [(LEV, ROWS, OWN)] * 3, [dots, initial_guess, p, w, q, s]))


def solution(mesh):
    lon, lat = mesh.shape["lon"], mesh.shape["lat"]
    z = 16 if lon % 16 == 0 else lon
    grid = jax.sharding.Mesh(mesh.devices.reshape(lon // z, z, lat), ("x", "z", "lat"))
    field = P(None, "lat", ("x", "z"))
    return jax.shard_map(
        shards, mesh=grid, in_specs=(field, field, field, P()), out_specs=(field, field, field), check_vma=False
    )
```
